32 devices in a mesh: tok: 8 (over y, x, core), head: 4 (over z).
Axes of the slice: x: 2, y: 2, z: 4, core: 2. Of those that a mesh axis runs over, the one named last changes fastest.
Arguments:
- queries: bfloat16 [32, 8192, 128], P('head', 'tok'), may hold values from -6 to 6
- keys: bfloat16 [4, 8192, 128], P('head', 'tok'), may hold values from -6 to 6
- values: bfloat16 [4, 8192, 128], P('head', 'tok'), may hold values from -6 to 6
- doc_lengths: int32 [8], replicated, may hold values from 1 to 4096, as said below
- tasks: int32 [128, 5], replicated, may hold values from 0 to 16, as said below
- w_out: bfloat16 [4096, 2048], P('head'), may hold values from -0.09375 to 0.09375
Outputs:
- projected: bfloat16 [8192, 2048], P('tok', 'head')
The draws below stay inside these ranges and needn't reach their ends.
Inputs may be any that keep to these rules, and one draw needn't show every extreme that they name: `doc_lengths`: the documents lie end to end; their lengths sum to 8192, and one is exactly 4096 tokens long. `tasks`: row t = qb * 8 + j describes query block qb (tokens qb * 512 to qb * 512 + 511) and head j of every group: column 0 is qb, column 1 is j, column 2 is the block that holds the first token of the document of the block's first token, column 3 is qb + 1, column 4 is the server, a token shard. Rows of one token shard's blocks name one server at most 2 times, 2 is reached, and every server is named in exactly 16 rows.
All inputs are finite; a program needn't handle non-finite values.
Results may differ from the reference program's by a relative error of at most 0.012.
Values may be sent and summed in bfloat16 or wider, within the bound.
No kernel may reach another device: no remote copies, remote signals or barrier semaphores. Data moves between devices by JAX's collectives and lax.ppermute only.
A program may use at most 128 MiB of HBM per device.

```python
import jax
import jax.numpy as jnp
from jax import lax

D = 2048
QH = 32
KVH = 4
HD = 128
QBLK = 512
HG = 8
TOKENS = 8192
BLK_DEV = 2
QB = 16
DOC_MOST = 4096
NDOC = 8
N_TOK = 8


def documents(key):
    seeded = jax.random.fold_in(key, 101)
    weights = jax.random.randint(jax.random.fold_in(seeded, 1), (NDOC,), 32, 64, dtype=jnp.int32)
    longest = jax.random.randint(jax.random.fold_in(seeded, 2), (), 0, NDOC, dtype=jnp.int32)
    doc_index = jnp.arange(NDOC, dtype=jnp.int32)
    is_longest = doc_index == longest
    weights = jnp.where(is_longest, 0, weights)
    spare = TOKENS - DOC_MOST - (NDOC - 1)
    shares = spare * weights // jnp.sum(weights)
    leftover = spare - jnp.sum(shares)
    target = jnp.where(longest == 0, 1, 0)
    shares = shares + jnp.where(doc_index == target, leftover, 0)
    return jnp.where(is_longest, DOC_MOST, shares + 1).astype(jnp.int32)


def draw_doc_lengths(key, part):
    return documents(key)


def draw_tasks(key, part):
    lengths = documents(key)
    starts = jnp.cumsum(lengths) - lengths
    block_ids = jnp.arange(QB, dtype=jnp.int32)
    first_rows = block_ids * QBLK
    doc_begin = jnp.max(jnp.where(starts[None, :] <= first_rows[:, None], starts[None, :], 0), axis=1)
    low_block = doc_begin // QBLK
    high_block = block_ids + 1
    device_cost = jnp.sum((high_block - low_block).reshape(N_TOK, BLK_DEV), axis=1)
    device_ids = jnp.arange(N_TOK, dtype=jnp.int32)
    ordering = jnp.argsort(-(device_cost * N_TOK + (N_TOK - 1 - device_ids)))
    ranking = jnp.zeros((N_TOK,), jnp.int32).at[ordering].set(device_ids)
    spread = 2 * ranking % N_TOK + 2 * ranking // N_TOK
    heads = jnp.arange(HG, dtype=jnp.int32)
    owner = block_ids // BLK_DEV
    within = block_ids % BLK_DEV
    unit_slot = heads[None, :] * BLK_DEV + within[:, None]
    server = (spread[owner][:, None] + unit_slot) % N_TOK
    columns = [jnp.broadcast_to(block_ids[:, None], (QB, HG)), jnp.broadcast_to(heads[None, :], (QB, HG)), jnp.broadcast_to(low_block[:, None], (QB, HG)), jnp.broadcast_to(high_block[:, None], (QB, HG)), server]
    return jnp.stack(columns, axis=-1).reshape(QB * HG, 5).astype(jnp.int32)


def draw_queries(key, part):
    drawn = jnp.clip(jax.random.normal(jax.random.fold_in(key, 1), (QH, TOKENS, HD), jnp.float32), -6.0, 6.0)
    return drawn.astype(jnp.bfloat16)


def draw_keys(key, part):
    drawn = jnp.clip(jax.random.normal(jax.random.fold_in(key, 3), (KVH, TOKENS, HD), jnp.float32), -6.0, 6.0)
    return drawn.astype(jnp.bfloat16)


def level_of(key, dims, pieces, least, largest):
    factor_of = 1.0
    for axis_at, parts in pieces:
        draws = jax.random.uniform(jax.random.fold_in(jax.random.fold_in(key, 6), axis_at), (parts,), jnp.float32, least / len(pieces), largest / len(pieces))
        factor_of = factor_of * jnp.repeat(jnp.exp(draws), dims[axis_at] // parts).reshape((-1,) + (1,) * (len(dims) - 1 - axis_at))
    return factor_of


def centred(key, dims, scale, bound, shards=(), held_as=jnp.bfloat16):
    loudness = level_of(key, dims, shards, -0.22, 0.18) if shards else 1.0
    drawn = jax.random.normal(key, dims, jnp.float32) * scale * loudness
    return jnp.minimum(jnp.maximum(drawn, -bound), bound).astype(held_as)


def setup_inputs(seed: int = 0) -> dict:
    streams_of = jax.random.split(jax.random.key(seed), 7)
    queries = draw_queries(jax.random.fold_in(streams_of[6], 71), 0)
    keys = draw_keys(jax.random.fold_in(streams_of[6], 71), 0)
    values = centred(streams_of[2], (KVH, TOKENS, HD), 1.0, 6.0, ((0, 4), (1, 8)))
    doc_lengths = draw_doc_lengths(jax.random.fold_in(streams_of[6], 71), 0)
    tasks = draw_tasks(jax.random.fold_in(streams_of[6], 71), 0)
    w_out = centred(streams_of[5], (QH * HD, D), (QH * HD) ** -0.5, 0.09375, ((0, 4),))
    return dict(queries=queries, keys=keys, values=values, doc_lengths=doc_lengths, tasks=tasks, w_out=w_out)


FLOOR_SCORE = -1e30


def reference(queries, keys, values, doc_lengths, tasks, w_out):
    starts = jnp.cumsum(doc_lengths) - doc_lengths
    scaling = 1.0 / (HD ** 0.5)
    stride = 2 * QBLK
    offsets = jnp.arange(stride, dtype=jnp.int32)
    head_rows = jnp.arange(HG, dtype=jnp.int32)

    def one_block(block_id):
        positions = block_id * QBLK + jnp.arange(QBLK, dtype=jnp.int32)
        doc_begin = jnp.max(jnp.where(starts[None, :] <= positions[:, None], starts[None, :], 0), axis=1)
        task_rows = block_id * HG + head_rows
        low_keys = tasks[task_rows, 2] * QBLK
        high_keys = tasks[task_rows, 3] * QBLK
        query_block = lax.dynamic_slice_in_dim(queries, (block_id * QBLK).astype(jnp.int32), QBLK, 1)
        query_block = query_block.astype(jnp.float32).reshape(KVH, HG, QBLK, HD)
        first_key = jnp.min(low_keys)
        last_key = jnp.max(high_keys)
        turn_count = (last_key - first_key + stride - 1) // stride

        def window(step_index):
            key_start = first_key + step_index * stride
            window_start = jnp.clip(key_start, 0, TOKENS - stride).astype(jnp.int32)
            key_block = lax.dynamic_slice_in_dim(keys, window_start, stride, 1).astype(jnp.float32)
            value_block = lax.dynamic_slice_in_dim(values, window_start, stride, 1).astype(jnp.float32)
            key_pos = window_start + offsets
            scores = jnp.einsum("ghqe,gke->ghqk", query_block, key_block) * scaling
            inside = (key_pos >= key_start) & (key_pos < key_start + stride)
            visible = inside[None, None, :] & (key_pos[None, None, :] >= low_keys[:, None, None])
            visible = visible & (key_pos[None, None, :] < high_keys[:, None, None])
            visible = visible & (key_pos[None, None, :] >= doc_begin[None, :, None])
            visible = visible & (key_pos[None, None, :] <= positions[None, :, None])
            return scores, visible[None], value_block

        def find_peak(step_index, running):
            scores, visible, unused = window(step_index)
            return jnp.maximum(running, jnp.max(jnp.where(visible, scores, FLOOR_SCORE), axis=-1))

        row_peak = lax.fori_loop(0, turn_count, find_peak, jnp.full((KVH, HG, QBLK), FLOOR_SCORE, jnp.float32))

        def add_window(step_index, carried):
            row_total, weighted = carried
            scores, visible, value_block = window(step_index)
            expo = jnp.where(visible, jnp.exp(scores - row_peak[..., None]), 0.0)
            row_total = row_total + jnp.sum(expo, axis=-1)
            rounded = lax.optimization_barrier(expo.astype(jnp.bfloat16)).astype(jnp.float32)
            weighted = weighted + jnp.einsum("ghqk,gke->ghqe", rounded, value_block)
            return row_total, weighted

        initial = (jnp.zeros((KVH, HG, QBLK), jnp.float32), jnp.zeros((KVH, HG, QBLK, HD), jnp.float32))
        row_total, weighted = lax.fori_loop(0, turn_count, add_window, initial)
        attended = (weighted / row_total[..., None]).astype(jnp.bfloat16)
        return attended.reshape(QH, QBLK, HD)

    blocks = lax.map(one_block, jnp.arange(QB, dtype=jnp.int32))
    attended = blocks.transpose(0, 2, 1, 3).reshape(TOKENS, QH * HD)
    return jnp.dot(attended, w_out, preferred_element_type=jnp.float32).astype(jnp.bfloat16)
```

```python
from functools import partial
import math

import jax
import jax.numpy as jnp
from jax import lax
from jax.experimental import pallas as pl
from jax.experimental.pallas import tpu as pltpu
from jax.sharding import PartitionSpec as P

FLOOR_SCORE = -1e30
CHUNKS = 4
LANES = 128


def attend_kernel(place, lengths, tasks, q_ref, *refs, spans, shard_rows, q_block, key_tile, pair):
    kv_refs = refs[: 2 * spans]
    out_ref, kv, acc, peak, total, q_split, sems = refs[2 * spans :]
    heads, rows, width = q_ref.shape
    units = heads // pair
    cols = pair * rows
    parity = place[0]
    copies = []
    for span in range(spans):
        for other in range(2):
            slot = 2 * span + (parity if other == 0 else 1 - parity)
            copy = pltpu.make_async_copy(
                kv_refs[2 * span + other], kv.at[slot], sems.at[2 * span + other]
            )
            copy.start()
            copies.append(copy)

    first_row = place[1]
    base = place[2]
    last_row = first_row + rows - 1
    one_head = first_row + lax.broadcasted_iota(jnp.int32, (1, rows), 1)
    begin = jnp.zeros((1, rows), jnp.int32)
    begin_first = jnp.int32(0)
    begin_last = jnp.int32(0)
    start = jnp.int32(0)
    for doc in range(lengths.shape[0]):
        begin = jnp.where(one_head >= start, jnp.maximum(begin, start), begin)
        begin_first = jnp.where(first_row >= start, jnp.maximum(begin_first, start), begin_first)
        begin_last = jnp.where(last_row >= start, jnp.maximum(begin_last, start), begin_last)
        start = start + lengths[doc]

    task = (first_row // q_block) * heads
    begins, ends = [], []
    low_least = low_most = high_least = high_most = None
    for head in range(heads):
        low = tasks[(task + head) * 5 + 2] * q_block
        high = tasks[(task + head) * 5 + 3] * q_block
        begins.append(jnp.maximum(begin, low))
        ends.append(jnp.minimum(one_head, high - 1))
        low_least = low if head == 0 else jnp.minimum(low_least, low)
        low_most = low if head == 0 else jnp.maximum(low_most, low)
        high_least = high if head == 0 else jnp.minimum(high_least, high)
        high_most = high if head == 0 else jnp.maximum(high_most, high)
    begins = [jnp.concatenate(begins[u * pair : (u + 1) * pair], axis=1) for u in range(units)]
    ends = [jnp.concatenate(ends[u * pair : (u + 1) * pair], axis=1) for u in range(units)]

    tiles = kv.shape[0] * shard_rows // key_tile
    lo = jnp.clip((jnp.maximum(low_least, begin_first) - base) // key_tile, 0, tiles)
    hi = jnp.clip(
        (jnp.minimum(high_most, last_row + 1) - base + key_tile - 1) // key_tile, lo, tiles
    )
    inner_lo = jnp.clip(
        (jnp.maximum(low_most, begin_last) - base + key_tile - 1) // key_tile, lo, hi
    )
    inner_hi = jnp.clip(
        (jnp.minimum(high_least, first_row + 1) - base) // key_tile, inner_lo, hi
    )

    acc[...] = jnp.zeros_like(acc)
    peak[...] = jnp.full_like(peak, FLOOR_SCORE)
    total[...] = jnp.zeros_like(total)
    factor = math.log2(math.e) / math.sqrt(width)
    for unit in range(units):
        scaled = q_ref[unit * pair : (unit + 1) * pair].reshape(cols, width).astype(jnp.float32)
        scaled = scaled * factor
        coarse = scaled.astype(jnp.bfloat16)
        q_split[unit, :, :width] = coarse
        q_split[unit, :, width:] = (scaled - coarse.astype(jnp.float32)).astype(jnp.bfloat16)
    for copy in copies:
        copy.wait()

    per_shard = shard_rows // key_tile

    def step(tile, masked):
        slot = tile // per_shard
        offset = pl.multiple_of((tile % per_shard) * key_tile, key_tile)
        keys = kv[slot, 0, pl.ds(offset, key_tile), :]
        keys = jnp.concatenate([keys, keys], axis=1)
        values = kv[slot, 1, pl.ds(offset, key_tile), :].T
        values = jnp.concatenate([values, jnp.ones((16, key_tile), jnp.bfloat16)], axis=0)
        key_pos = (
            base + tile * key_tile + lax.broadcasted_iota(jnp.int32, (key_tile, 1), 0)
            if masked
            else None
        )

        def scores_of(unit):
            return lax.dot_general(
                keys,
                q_split[unit],
                (((1,), (1,)), ((), ())),
                preferred_element_type=jnp.float32,
            )

        def weigh(unit, scores):
            if masked:
                visible = (key_pos >= begins[unit]) & (key_pos <= ends[unit])
                scores = jnp.where(visible, scores, FLOOR_SCORE)
            before = peak[unit]
            now = jnp.maximum(before, jnp.max(scores, axis=0, keepdims=True))
            peak[unit] = now
            return jnp.exp2(scores - now).astype(jnp.bfloat16), jnp.exp2(before - now)

        def gather(unit, weights, rescale):
            product = lax.dot_general(
                values, weights, (((1,), (0,)), ((), ())), preferred_element_type=jnp.float32
            )
            total[unit] = total[unit] * rescale + product[width : width + 1]
            acc[unit] = acc[unit] * rescale + product[:width]

        scores = scores_of(0)
        waiting = None
        for unit in range(units):
            ahead = scores_of(unit + 1) if unit + 1 < units else None
            weighed = weigh(unit, scores)
            if waiting is not None:
                gather(unit - 1, *waiting)
            waiting, scores = weighed, ahead
        gather(units - 1, *waiting)

    def inner(tile, carried):
        step(tile, False)
        return carried

    def edge(turn, carried):
        step(jnp.where(turn < inner_lo - lo, lo + turn, inner_hi + turn - (inner_lo - lo)), True)
        return carried

    lax.fori_loop(inner_lo, inner_hi, inner, 0)
    lax.fori_loop(0, (inner_lo - lo) + (hi - inner_hi), edge, 0)
    for unit in range(units):
        done = (acc[unit] / total[unit]).T.astype(jnp.bfloat16)
        for member in range(pair):
            head = unit * pair + member
            out_ref[:, head * width : (head + 1) * width] = done[member * rows : (member + 1) * rows]


def attend(place, lengths, tasks, queries, kvs, chunk, rows, q_block):
    heads, _, width = queries.shape
    _, shard_rows, _ = kvs[0].shape
    slots = len(kvs)
    pair = max(1, min(heads, 512 // rows))
    key_tile = min(512, shard_rows)
    units, cols = heads // pair, pair * rows
    return pl.pallas_call(
        partial(
            attend_kernel,
            spans=slots // 2,
            shard_rows=shard_rows,
            q_block=q_block,
            key_tile=key_tile,
            pair=pair,
        ),
        grid_spec=pltpu.PrefetchScalarGridSpec(
            num_scalar_prefetch=3,
            grid=(1,),
            in_specs=[pl.BlockSpec((heads, rows, width), lambda i, *_: (0, chunk, 0))]
            + [pl.BlockSpec(memory_space=pl.ANY)] * slots,
            out_specs=pl.BlockSpec((rows, heads * width), lambda i, *_: (0, 0)),
            scratch_shapes=[
                pltpu.VMEM((slots, 2, shard_rows, width), jnp.bfloat16),
                pltpu.VMEM((units, width, cols), jnp.float32),
                pltpu.VMEM((units, 1, cols), jnp.float32),
                pltpu.VMEM((units, 1, cols), jnp.float32),
                pltpu.VMEM((units, cols, 2 * width), jnp.bfloat16),
                pltpu.SemaphoreType.DMA((slots,)),
            ],
        ),
        out_shape=jax.ShapeDtypeStruct((rows, heads * width), jnp.bfloat16),
        compiler_params=pltpu.CompilerParams(vmem_limit_bytes=48 * 2**20),
        cost_estimate=pl.CostEstimate(
            flops=heads * rows * 4096 * width * 4,
            bytes_accessed=8 * 2**20,
            transcendentals=heads * rows * 4096,
        ),
    )(place, lengths, tasks, queries, *kvs)


def local(queries, keys, values, doc_lengths, tasks, w_out):
    heads, tok_dev, width = queries.shape
    n_tok = lax.axis_size("tok")
    n_head = lax.axis_size("head")
    me = lax.axis_index("tok")
    tokens = n_tok * tok_dev
    q_block = tokens * heads // tasks.shape[0]
    chips = n_tok // 2
    doc_most = tokens * 4 // doc_lengths.shape[0]
    back = min(chips - 1, -(-(doc_most - 1) // (2 * tok_dev)))

    own = jnp.concatenate([keys, values], axis=0)
    spans = []
    for hop in range(back, 0, -1):
        pairs = [(i, i + 2 * hop) for i in range(n_tok - 2 * hop)]
        spans.append(lax.ppermute(own, "tok", pairs))
    spans.append(own)
    swap = [(i, i ^ 1) for i in range(n_tok)]
    kvs = []
    for mine in spans:
        kvs += [mine, lax.ppermute(mine, "tok", swap)]

    z = lax.axis_index("head")
    out_cols = w_out.shape[1] // n_head
    flat_tasks = tasks.reshape(-1)
    rows = tok_dev // CHUNKS
    base = (me // 2 - back) * 2 * tok_dev

    def column(block):
        return lax.dynamic_slice_in_dim(w_out, block * out_cols, out_cols, 1)

    w_send = jnp.concatenate([column((z ^ 1) ^ 2), column(z ^ 1)], axis=1)
    w_keep = jnp.concatenate([column(z ^ 2), column(z)], axis=1)
    near = [(i, i ^ 1) for i in range(n_head)]
    far = [(i, i ^ 2) for i in range(n_head)]
    outs = []
    for chunk in range(CHUNKS):
        place = jnp.stack([me % 2, me * tok_dev + chunk * rows, base]).astype(jnp.int32)
        attended = attend(place, doc_lengths, flat_tasks, queries, kvs, chunk, rows, q_block)
        sent = jnp.dot(attended, w_send, preferred_element_type=jnp.float32)
        arrived = lax.ppermute(sent.astype(jnp.bfloat16), "head", near)
        kept = jnp.dot(attended, w_keep, preferred_element_type=jnp.float32)
        summed = kept + arrived.astype(jnp.float32)
        crossed = lax.ppermute(summed[:, :out_cols].astype(jnp.bfloat16), "head", far)
        outs.append((summed[:, out_cols:] + crossed.astype(jnp.float32)).astype(jnp.bfloat16))
    return jnp.concatenate(outs, axis=0)


def solution(mesh):
    placed = (
        P("head", "tok", None),
        P("head", "tok", None),
        P("head", "tok", None),
        P(),
        P(),
        P("head", None),
    )
    return jax.shard_map(
        local, mesh=mesh, in_specs=placed, out_specs=P("tok", "head"), check_vma=False
    )
```

```python
from functools import partial
import math

import jax
import jax.numpy as jnp
from jax import lax
from jax.experimental import pallas as pl
from jax.experimental.pallas import tpu as pltpu
from jax.sharding import PartitionSpec as P

FLOOR_SCORE = -1e30
CHUNKS = 4
LANES = 128


def attend_kernel(place, lengths, tasks, q_ref, *refs, spans, shard_rows, q_block, key_tile, pair):
    kv_refs = refs[: 2 * spans]
    out_ref, kv, acc, peak, total, q_split, sems = refs[2 * spans :]
    heads, rows, width = q_ref.shape
    units = heads // pair
    cols = pair * rows
    parity = place[0]
    copies = []
    for span in range(spans):
        for other in range(2):
            slot = 2 * span + (parity if other == 0 else 1 - parity)
            copy = pltpu.make_async_copy(
                kv_refs[2 * span + other], kv.at[slot], sems.at[2 * span + other]
            )
            copy.start()
            copies.append(copy)

    first_row = place[1]
    base = place[2]
    last_row = first_row + rows - 1
    one_head = first_row + lax.broadcasted_iota(jnp.int32, (1, rows), 1)
    begin = jnp.zeros((1, rows), jnp.int32)
    begin_first = jnp.int32(0)
    begin_last = jnp.int32(0)
    start = jnp.int32(0)
    for doc in range(lengths.shape[0]):
        begin = jnp.where(one_head >= start, jnp.maximum(begin, start), begin)
        begin_first = jnp.where(first_row >= start, jnp.maximum(begin_first, start), begin_first)
        begin_last = jnp.where(last_row >= start, jnp.maximum(begin_last, start), begin_last)
        start = start + lengths[doc]

    task = (first_row // q_block) * heads
    begins, ends = [], []
    low_least = low_most = high_least = high_most = None
    for head in range(heads):
        low = tasks[(task + head) * 5 + 2] * q_block
        high = tasks[(task + head) * 5 + 3] * q_block
        begins.append(jnp.maximum(begin, low))
        ends.append(jnp.minimum(one_head, high - 1))
        low_least = low if head == 0 else jnp.minimum(low_least, low)
        low_most = low if head == 0 else jnp.maximum(low_most, low)
        high_least = high if head == 0 else jnp.minimum(high_least, high)
        high_most = high if head == 0 else jnp.maximum(high_most, high)
    begins = [jnp.concatenate(begins[u * pair : (u + 1) * pair], axis=1) for u in range(units)]
    ends = [jnp.concatenate(ends[u * pair : (u + 1) * pair], axis=1) for u in range(units)]

    tiles = kv.shape[0] * shard_rows // key_tile
    lo = jnp.clip((jnp.maximum(low_least, begin_first) - base) // key_tile, 0, tiles)
    hi = jnp.clip(
        (jnp.minimum(high_most, last_row + 1) - base + key_tile - 1) // key_tile, lo, tiles
    )
    inner_lo = jnp.clip(
        (jnp.maximum(low_most, begin_last) - base + key_tile - 1) // key_tile, lo, hi
    )
    inner_hi = jnp.clip(
        (jnp.minimum(high_least, first_row + 1) - base) // key_tile, inner_lo, hi
    )

    acc[...] = jnp.zeros_like(acc)
    peak[...] = jnp.full_like(peak, FLOOR_SCORE)
    total[...] = jnp.zeros_like(total)
    factor = math.log2(math.e) / math.sqrt(width)
    for unit in range(units):
        scaled = q_ref[unit * pair : (unit + 1) * pair].reshape(cols, width).astype(jnp.float32)
        scaled = scaled * factor
        coarse = scaled.astype(jnp.bfloat16)
        q_split[unit, :, :width] = coarse
        q_split[unit, :, width:] = (scaled - coarse.astype(jnp.float32)).astype(jnp.bfloat16)
    for copy in copies:
        copy.wait()

    per_shard = shard_rows // key_tile

    def step(tile, masked):
        slot = tile // per_shard
        offset = pl.multiple_of((tile % per_shard) * key_tile, key_tile)
        keys = kv[slot, 0, pl.ds(offset, key_tile), :]
        keys = jnp.concatenate([keys, keys], axis=1)
        values = kv[slot, 1, pl.ds(offset, key_tile), :].T
        values = jnp.concatenate([values, jnp.ones((16, key_tile), jnp.bfloat16)], axis=0)
        key_pos = (
            base + tile * key_tile + lax.broadcasted_iota(jnp.int32, (key_tile, 1), 0)
            if masked
            else None
        )

        def scores_of(unit):
            return lax.dot_general(
                keys,
                q_split[unit],
                (((1,), (1,)), ((), ())),
                preferred_element_type=jnp.float32,
            )

        def weigh(unit, scores):
            if masked:
                visible = (key_pos >= begins[unit]) & (key_pos <= ends[unit])
                scores = jnp.where(visible, scores, FLOOR_SCORE)
            before = peak[unit]
            now = jnp.maximum(before, jnp.max(scores, axis=0, keepdims=True))
            peak[unit] = now
            return jnp.exp2(scores - now).astype(jnp.bfloat16), jnp.exp2(before - now)

        def gather(unit, weights, rescale):
            product = lax.dot_general(
                values, weights, (((1,), (0,)), ((), ())), preferred_element_type=jnp.float32
            )
            total[unit] = total[unit] * rescale + product[width : width + 1]
            acc[unit] = acc[unit] * rescale + product[:width]

        scores = scores_of(0)
        waiting = None
        for unit in range(units):
            ahead = scores_of(unit + 1) if unit + 1 < units else None
            weighed = weigh(unit, scores)
            if waiting is not None:
                gather(unit - 1, *waiting)
            waiting, scores = weighed, ahead
        gather(units - 1, *waiting)

    def inner(tile, carried):
        step(tile, False)
        return carried

    def edge(turn, carried):
        step(jnp.where(turn < inner_lo - lo, lo + turn, inner_hi + turn - (inner_lo - lo)), True)
        return carried

    lax.fori_loop(inner_lo, inner_hi, inner, 0)
    lax.fori_loop(0, (inner_lo - lo) + (hi - inner_hi), edge, 0)
    for unit in range(units):
        done = (acc[unit] / total[unit]).T.astype(jnp.bfloat16)
        for member in range(pair):
            head = unit * pair + member
            out_ref[:, head * width : (head + 1) * width] = done[member * rows : (member + 1) * rows]


def attend(place, lengths, tasks, queries, kvs, chunk, rows, q_block):
    heads, _, width = queries.shape
    _, shard_rows, _ = kvs[0].shape
    slots = len(kvs)
    pair = max(1, min(heads, 512 // rows))
    key_tile = min(512, shard_rows)
    units, cols = heads // pair, pair * rows
    return pl.pallas_call(
        partial(
            attend_kernel,
            spans=slots // 2,
            shard_rows=shard_rows,
            q_block=q_block,
            key_tile=key_tile,
            pair=pair,
        ),
        grid_spec=pltpu.PrefetchScalarGridSpec(
            num_scalar_prefetch=3,
            grid=(1,),
            in_specs=[pl.BlockSpec((heads, rows, width), lambda i, *_: (0, chunk, 0))]
            + [pl.BlockSpec(memory_space=pl.ANY)] * slots,
            out_specs=pl.BlockSpec((rows, heads * width), lambda i, *_: (0, 0)),
            scratch_shapes=[
                pltpu.VMEM((slots, 2, shard_rows, width), jnp.bfloat16),
                pltpu.VMEM((units, width, cols), jnp.float32),
                pltpu.VMEM((units, 1, cols), jnp.float32),
                pltpu.VMEM((units, 1, cols), jnp.float32),
                pltpu.VMEM((units, cols, 2 * width), jnp.bfloat16),
                pltpu.SemaphoreType.DMA((slots,)),
            ],
        ),
        out_shape=jax.ShapeDtypeStruct((rows, heads * width), jnp.bfloat16),
        compiler_params=pltpu.CompilerParams(vmem_limit_bytes=48 * 2**20),
        cost_estimate=pl.CostEstimate(
            flops=heads * rows * 4096 * width * 4,
            bytes_accessed=8 * 2**20,
            transcendentals=heads * rows * 4096,
        ),
    )(place, lengths, tasks, queries, *kvs)


def local(queries, keys, values, doc_lengths, tasks, w_out):
    heads, tok_dev, width = queries.shape
    n_tok = lax.axis_size("tok")
    n_head = lax.axis_size("head")
    me = lax.axis_index("tok")
    tokens = n_tok * tok_dev
    q_block = tokens * heads // tasks.shape[0]
    chips = n_tok // 2
    doc_most = tokens * 4 // doc_lengths.shape[0]
    back = min(chips - 1, -(-(doc_most - 1) // (2 * tok_dev)))

    own = jnp.concatenate([keys, values], axis=0)
    spans = []
    for hop in range(back, 0, -1):
        pairs = [(i, i + 2 * hop) for i in range(n_tok - 2 * hop)]
        spans.append(lax.ppermute(own, "tok", pairs))
    spans.append(own)

    z = lax.axis_index("head")
    out_cols = w_out.shape[1] // n_head
    flat_tasks = tasks.reshape(-1)
    rows = tok_dev // CHUNKS
    base = (me // 2 - back) * 2 * tok_dev

    def column(block):
        return lax.dynamic_slice_in_dim(w_out, block * out_cols, out_cols, 1)

    w_send = jnp.concatenate([column((z ^ 1) ^ 2), column(z ^ 1)], axis=1)
    w_keep = jnp.concatenate([column(z ^ 2), column(z)], axis=1)
    near = [(i, i ^ 1) for i in range(n_head)]
    far = [(i, i ^ 2) for i in range(n_head)]
    spans, w_send, w_keep, flat_tasks = lax.optimization_barrier(
        (spans, w_send, w_keep, flat_tasks)
    )
    swap = [(i, i ^ 1) for i in range(n_tok)]
    kvs = []
    for mine in spans:
        kvs += [mine, lax.ppermute(mine, "tok", swap)]

    def project(attended):
        sent = jnp.dot(attended, w_send, preferred_element_type=jnp.float32)
        return sent.astype(jnp.bfloat16)

    def hop(attended, arrived):
        kept = jnp.dot(attended, w_keep, preferred_element_type=jnp.float32)
        summed = kept + arrived.astype(jnp.float32)
        return summed[:, :out_cols].astype(jnp.bfloat16), summed[:, out_cols:]

    halves = []
    attended = sent = summed = None
    for chunk in range(CHUNKS):
        place = jnp.stack([me % 2, me * tok_dev + chunk * rows, base]).astype(jnp.int32)
        place, sent, summed = lax.optimization_barrier((place, sent, summed))
        arrived = None if sent is None else lax.ppermute(sent, "head", near)
        crossed = None if summed is None else lax.ppermute(summed[0], "head", far)
        ready = attend(place, doc_lengths, flat_tasks, queries, kvs, chunk, rows, q_block)
        sent, arrived, crossed = lax.optimization_barrier((project(ready), arrived, crossed))
        if crossed is not None:
            halves.append((summed[1], crossed))
        summed = None if arrived is None else hop(attended, arrived)
        attended = ready
    arrived = lax.ppermute(sent, "head", near)
    if summed is not None:
        halves.append((summed[1], lax.ppermute(summed[0], "head", far)))
    summed = hop(attended, arrived)
    halves.append((summed[1], lax.ppermute(summed[0], "head", far)))
    outs = [(held + crossed.astype(jnp.float32)).astype(jnp.bfloat16) for held, crossed in halves]
    return jnp.concatenate(outs, axis=0)


def solution(mesh):
    placed = (
        P("head", "tok", None),
        P("head", "tok", None),
        P("head", "tok", None),
        P(),
        P(),
        P("head", None),
    )
    return jax.shard_map(
        local, mesh=mesh, in_specs=placed, out_specs=P("tok", "head"), check_vma=False
    )
```

```python
from functools import partial
import math

import jax
import jax.numpy as jnp
from jax import lax
from jax.experimental import pallas as pl
from jax.experimental.pallas import tpu as pltpu
from jax.sharding import PartitionSpec as P

FLOOR_SCORE = -1e30
CHUNKS = 4
SAFE_TOTAL = 2.0**100
KEY_TILE = 512
EDGE_TILE = 256


def attend_kernel(place, lengths, tasks, q_ref, *refs, spans, shard_rows, q_block, key_tile, edge_tile, pair, resume, suspend):
    key_refs, value_refs, refs = refs[: 2 * spans], refs[2 * spans : 4 * spans], refs[4 * spans :]
    states, refs = (refs[:3], refs[3:]) if resume else (None, refs)
    outs, refs = (refs[:3], refs[3:]) if suspend else (refs[:1], refs[1:])
    key_all, value_all, acc, peak, total, s_buf, p_buf, rescale_buf, sems = refs
    heads, rows, width = q_ref.shape
    units = heads // pair
    cols = pair * rows
    parity = place[0]
    copies = []

    for span in range(spans):
        for other in range(2):
            at = 2 * span + other
            slot = 2 * span + (parity if other == 0 else 1 - parity)
            copies.append(pltpu.make_async_copy(key_refs[at], key_all.at[slot], sems.at[2 * at]))
            copies.append(
                pltpu.make_async_copy(value_refs[at], value_all.at[slot], sems.at[2 * at + 1])
            )

    def fetch():
        for copy in copies:
            copy.start()

    if suspend:
        pl.when(pl.program_id(0) == 0)(fetch)
    else:
        fetch()

    first_row = place[1] + pl.program_id(0) * rows
    base = place[2]
    last_row = first_row + rows - 1
    one_head = first_row + lax.broadcasted_iota(jnp.int32, (1, rows), 1)
    begin = jnp.zeros((1, rows), jnp.int32)
    begin_first = jnp.int32(0)
    begin_last = jnp.int32(0)
    start = jnp.int32(0)
    for doc in range(lengths.shape[0]):
        begin = jnp.where(one_head >= start, jnp.maximum(begin, start), begin)
        begin_first = jnp.where(first_row >= start, jnp.maximum(begin_first, start), begin_first)
        begin_last = jnp.where(last_row >= start, jnp.maximum(begin_last, start), begin_last)
        start = start + lengths[doc]

    task = (first_row // q_block) * heads
    begins, ends = [], []
    low_least = low_most = high_least = high_most = None
    for head in range(heads):
        low = tasks[(task + head) * 5 + 2] * q_block
        high = tasks[(task + head) * 5 + 3] * q_block
        begins.append(jnp.maximum(begin, low))
        ends.append(jnp.minimum(one_head, high - 1))
        low_least = low if head == 0 else jnp.minimum(low_least, low)
        low_most = low if head == 0 else jnp.maximum(low_most, low)
        high_least = high if head == 0 else jnp.minimum(high_least, high)
        high_most = high if head == 0 else jnp.maximum(high_most, high)
    begins = [jnp.concatenate(begins[u * pair : (u + 1) * pair], axis=1) for u in range(units)]
    ends = [jnp.concatenate(ends[u * pair : (u + 1) * pair], axis=1) for u in range(units)]

    ratio = key_tile // edge_tile
    tiles = 2 * spans * shard_rows // edge_tile
    lo = jnp.clip((jnp.maximum(low_least, begin_first) - base) // edge_tile, 0, tiles)
    hi = jnp.clip(
        (jnp.minimum(high_most, last_row + 1) - base + edge_tile - 1) // edge_tile, lo, tiles
    )
    full_lo = (jnp.maximum(low_most, begin_last) - base + key_tile - 1) // key_tile
    full_hi = (jnp.minimum(high_least, first_row + 1) - base) // key_tile
    full_lo = jnp.clip(full_lo, 0, tiles // ratio)
    full_hi = jnp.minimum(full_hi, tiles // ratio)
    some = full_hi > full_lo
    inner_lo = jnp.where(some, full_lo * ratio, lo)
    inner_hi = jnp.where(some, full_hi * ratio, lo)

    def reset():
        if resume:
            acc[...] = states[0][...].reshape(acc.shape)
            peak[...] = states[1][...].reshape(peak.shape)
            total[...] = states[2][...].reshape(total.shape)
        else:
            acc[...] = jnp.zeros_like(acc)
            peak[...] = jnp.full_like(peak, FLOOR_SCORE)
            total[...] = jnp.zeros_like(total)

    reset()
    factor = math.log2(math.e) / math.sqrt(width)

    def wait():
        for copy in copies:
            copy.wait()

    if suspend:
        pl.when(pl.program_id(0) == 0)(wait)
    else:
        wait()

    def sweep(count, tile_of, size, masked, fixed):
        per_shard = shard_rows // size

        def keys_of(tile):
            offset = pl.multiple_of((tile % per_shard) * size, size)
            return key_all[tile // per_shard, pl.ds(offset, size), :]

        def values_of(tile):
            offset = pl.multiple_of((tile % per_shard) * size, size)
            values = value_all[tile // per_shard, :, pl.ds(offset, size)]
            return jnp.concatenate([values, jnp.ones((16, size), jnp.bfloat16)], axis=0)

        def scores_of(keys, unit):
            return lax.dot_general(
                keys,
                q_ref[unit * pair : (unit + 1) * pair].reshape(cols, width),
                (((1,), (1,)), ((), ())),
                preferred_element_type=jnp.float32,
            )

        def gather(values, unit, weights, rescale):
            product = lax.dot_general(
                values, weights, (((1,), (0,)), ((), ())), preferred_element_type=jnp.float32
            )
            if fixed:
                total[unit] += product[width : width + 1]
                acc[unit] += product[:width]
            else:
                total[unit] = total[unit] * rescale + product[width : width + 1]
                acc[unit] = acc[unit] * rescale + product[:width]

        def step(turn, carried):
            tile = tile_of(turn)
            keys, values = keys_of(tile), values_of(tile)
            key_pos = (
                base + tile * size + lax.broadcasted_iota(jnp.int32, (size, 1), 0)
                if masked
                else None
            )
            scores = s_buf[:size]
            waiting = None
            for unit in range(units):
                if unit + 1 < units:
                    ahead = scores_of(keys, unit + 1)
                else:
                    ahead = scores_of(keys_of(tile_of(jnp.minimum(turn + 1, count - 1))), 0)
                if masked:
                    visible = (key_pos >= begins[unit]) & (key_pos <= ends[unit])
                    scores = jnp.where(visible, scores, FLOOR_SCORE)
                before = peak[unit]
                if fixed:
                    now, rescale = before, None
                else:
                    now = jnp.maximum(before, jnp.max(scores, axis=0, keepdims=True) * factor)
                    peak[unit] = now
                    rescale = jnp.exp2(before - now)
                weights = jnp.exp2(scores * factor - now).astype(jnp.bfloat16)
                if waiting is not None:
                    gather(values, unit - 1, *waiting)
                else:
                    earlier = values_of(tile_of(jnp.maximum(turn - 1, 0)))
                    gather(earlier, units - 1, p_buf[:size], rescale_buf[...])
                waiting = weights, rescale
                scores = ahead
            s_buf[:size] = scores
            p_buf[:size] = waiting[0]
            if not fixed:
                rescale_buf[...] = waiting[1]
            return carried

        def whole():
            p_buf[:size] = jnp.zeros((size, cols), jnp.bfloat16)
            rescale_buf[...] = jnp.ones_like(rescale_buf)
            s_buf[:size] = scores_of(keys_of(tile_of(0)), 0)
            lax.fori_loop(0, count, step, 0)
            gather(values_of(tile_of(count - 1)), units - 1, p_buf[:size], rescale_buf[...])

        pl.when(count > 0)(whole)

    sweep(
        (inner_hi - inner_lo) // ratio,
        lambda turn: inner_lo // ratio + turn,
        key_tile,
        False,
        resume,
    )
    left = inner_lo - lo
    sweep(
        left + hi - inner_hi,
        lambda turn: jnp.where(turn < left, lo + turn, inner_hi + turn - left),
        edge_tile,
        True,
        resume,
    )
    if resume:
        in_range = jnp.min(jnp.where(total[...] < SAFE_TOTAL, 1.0, 0.0))

        @pl.when(in_range < 0.5)
        def again():
            reset()
            sweep(hi - lo, lambda turn: lo + turn, edge_tile, True, False)

    if suspend:
        outs[0][...] = acc[...].reshape(outs[0].shape)
        outs[1][...] = peak[...].reshape(outs[1].shape)
        outs[2][...] = total[...].reshape(outs[2].shape)
        return
    for unit in range(units):
        done = (acc[unit] / total[unit]).T.astype(jnp.bfloat16)
        for member in range(pair):
            head = unit * pair + member
            outs[0][:, head * width : (head + 1) * width] = done[member * rows : (member + 1) * rows]


def attend(place, lengths, tasks, queries, kvs, chunk, rows, q_block, states=None, suspend=False):
    heads, tok_dev, width = queries.shape
    shard_rows = kvs[0][0].shape[0]
    slots = len(kvs)
    pair = max(1, min(heads, 512 // rows))
    key_tile = min(KEY_TILE, shard_rows)
    edge_tile = min(EDGE_TILE, key_tile)
    units, cols = heads // pair, pair * rows
    state_shapes = [(units, width, cols), (units, 1, cols), (units, 1, cols)]

    def at_chunk(shape):
        return pl.BlockSpec((1,) + shape, lambda i, *_: (chunk + i, 0, 0, 0))

    in_specs = [pl.BlockSpec((heads, rows, width), lambda i, *_: (0, chunk + i, 0))]
    in_specs += [pl.BlockSpec(memory_space=pl.ANY)] * (2 * slots)
    if states is not None:
        in_specs += [at_chunk(shape) for shape in state_shapes]
    steps = tok_dev // rows if suspend else 1
    if suspend:
        out_specs = [at_chunk(shape) for shape in state_shapes]
        out_shape = [jax.ShapeDtypeStruct((steps,) + shape, jnp.float32) for shape in state_shapes]
    else:
        out_specs = pl.BlockSpec((rows, heads * width), lambda i, *_: (0, 0))
        out_shape = jax.ShapeDtypeStruct((rows, heads * width), jnp.bfloat16)
    return pl.pallas_call(
        partial(
            attend_kernel,
            spans=slots // 2,
            shard_rows=shard_rows,
            q_block=q_block,
            key_tile=key_tile,
            edge_tile=edge_tile,
            pair=pair,
            resume=states is not None,
            suspend=suspend,
        ),
        grid_spec=pltpu.PrefetchScalarGridSpec(
            num_scalar_prefetch=3,
            grid=(steps,),
            in_specs=in_specs,
            out_specs=out_specs,
            scratch_shapes=[
                pltpu.VMEM((slots, shard_rows, width), jnp.bfloat16),
                pltpu.VMEM((slots, width, shard_rows), jnp.bfloat16),
                pltpu.VMEM((units, width, cols), jnp.float32),
                pltpu.VMEM((units, 1, cols), jnp.float32),
                pltpu.VMEM((units, 1, cols), jnp.float32),
                pltpu.VMEM((key_tile, cols), jnp.float32),
                pltpu.VMEM((key_tile, cols), jnp.bfloat16),
                pltpu.VMEM((1, cols), jnp.float32),
                pltpu.SemaphoreType.DMA((2 * slots,)),
            ],
        ),
        out_shape=out_shape,
        compiler_params=pltpu.CompilerParams(vmem_limit_bytes=48 * 2**20),
        cost_estimate=pl.CostEstimate(
            flops=heads * rows * 4096 * width * 4,
            bytes_accessed=8 * 2**20,
            transcendentals=heads * rows * 4096,
        ),
    )(place, lengths, tasks, queries, *[k for k, _ in kvs], *[v for _, v in kvs], *(states or ()))


def local(queries, keys, values, doc_lengths, tasks, w_out):
    heads, tok_dev, width = queries.shape
    n_tok = lax.axis_size("tok")
    n_head = lax.axis_size("head")
    me = lax.axis_index("tok")
    tokens = n_tok * tok_dev
    q_block = tokens * heads // tasks.shape[0]
    chips = n_tok // 2
    doc_most = tokens * 4 // doc_lengths.shape[0]
    back = min(chips - 1, -(-(doc_most - 1) // (2 * tok_dev)))

    own = keys[0], values[0].T
    spans = []
    for hop in range(back, 0, -1):
        pairs = [(i, i + 2 * hop) for i in range(n_tok - 2 * hop)]
        spans.append(tuple(lax.ppermute(part, "tok", pairs) for part in own))
    swap = [(i, i ^ 1) for i in range(n_tok)]
    beside = [own, tuple(lax.ppermute(part, "tok", swap) for part in own)]

    z = lax.axis_index("head")
    out_cols = w_out.shape[1] // n_head
    flat_tasks = tasks.reshape(-1)
    rows = tok_dev // CHUNKS
    base = (me // 2 - back) * 2 * tok_dev

    def column(block):
        return lax.dynamic_slice_in_dim(w_out, block * out_cols, out_cols, 1)

    w_send = jnp.concatenate([column((z ^ 1) ^ 2), column(z ^ 1)], axis=1)
    w_keep = jnp.concatenate([column(z ^ 2), column(z)], axis=1)
    near = [(i, i ^ 1) for i in range(n_head)]
    far = [(i, i ^ 2) for i in range(n_head)]
    w_send, w_keep, flat_tasks, beside = lax.optimization_barrier(
        (w_send, w_keep, flat_tasks, beside)
    )
    chip_start = (me // 2) * 2 * tok_dev
    place = jnp.stack([me % 2, me * tok_dev, chip_start]).astype(jnp.int32)
    states = attend(
        place, doc_lengths, flat_tasks, queries, beside, 0, rows, q_block, suspend=True
    )
    spans, states = lax.optimization_barrier((spans, states))
    kvs = []
    for mine in spans:
        kvs += [mine, tuple(lax.ppermute(part, "tok", swap) for part in mine)]

    def project(attended):
        sent = jnp.dot(attended, w_send, preferred_element_type=jnp.float32)
        return sent.astype(jnp.bfloat16)

    def hop(attended, arrived):
        kept = jnp.dot(attended, w_keep, preferred_element_type=jnp.float32)
        summed = kept + arrived.astype(jnp.float32)
        return summed[:, :out_cols].astype(jnp.bfloat16), summed[:, out_cols:]

    halves = []
    attended = sent = summed = None
    for chunk in range(CHUNKS):
        place = jnp.stack([me % 2, me * tok_dev + chunk * rows, base]).astype(jnp.int32)
        place, sent, summed = lax.optimization_barrier((place, sent, summed))
        arrived = None if sent is None else lax.ppermute(sent, "head", near)
        crossed = None if summed is None else lax.ppermute(summed[0], "head", far)
        ready = attend(place, doc_lengths, flat_tasks, queries, kvs, chunk, rows, q_block, states)
        sent, arrived, crossed = lax.optimization_barrier((project(ready), arrived, crossed))
        if crossed is not None:
            halves.append((summed[1], crossed))
        summed = None if arrived is None else hop(attended, arrived)
        attended = ready
    arrived = lax.ppermute(sent, "head", near)
    if summed is not None:
        halves.append((summed[1], lax.ppermute(summed[0], "head", far)))
    summed = hop(attended, arrived)
    halves.append((summed[1], lax.ppermute(summed[0], "head", far)))
    outs = [(held + crossed.astype(jnp.float32)).astype(jnp.bfloat16) for held, crossed in halves]
    return jnp.concatenate(outs, axis=0)


def solution(mesh):
    placed = (
        P("head", "tok", None),
        P("head", "tok", None),
        P("head", "tok", None),
        P(),
        P(),
        P("head", None),
    )
    return jax.shard_map(
        local, mesh=mesh, in_specs=placed, out_specs=P("tok", "head"), check_vma=False
    )
```

```python
from functools import partial
import math

import jax
import jax.numpy as jnp
from jax import lax
from jax.experimental import pallas as pl
from jax.experimental.pallas import tpu as pltpu
from jax.sharding import PartitionSpec as P

FLOOR_SCORE = -1e30
SAFE_TOTAL = 2.0**100
KEY_TILE = 512
EDGE_TILE = 256
SUB = 128
PAIR = 4
FIRST_PARTS = 4
PARTS = (1, 2, 2, 2, 1)


def attend_kernel(
    place, lengths, tasks, q_ref, *refs, slots, subs, q_block, key_tile, edge_tile, resume
):
    key_refs, value_refs, refs = refs[:slots], refs[slots : 2 * slots], refs[2 * slots :]
    if resume:
        states, w_ref, refs = refs[:3], refs[3], refs[4:]
        sent_ref, kept_ref, q_buf, key_all, value_all, acc, peak, total = refs[:8]
        s_buf, p_buf, rescale_buf, sems, w_buf, attended, w_sems = refs[8:]
    else:
        outs, refs = refs[:3], refs[3:]
        q_buf, key_all, value_all, acc, peak, total, s_buf, p_buf, rescale_buf, sems = refs
    heads, _, width = q_ref.shape
    shard_rows = key_refs[0].shape[0]
    groups = heads // PAIR
    units = subs * groups
    cols = PAIR * SUB
    rows = subs * SUB
    step_id = pl.program_id(0)
    parity = place[0]
    first_row = place[1] + step_id * rows
    base = place[2]
    limit = place[3]
    local_row = place[4] + step_id * rows

    q_copy = pltpu.make_async_copy(
        q_ref.at[:, pl.ds(pl.multiple_of(local_row, SUB), rows), :], q_buf, sems.at[2 * slots]
    )
    q_copy.start()
    copies = []
    for at in range(slots):
        slot = at if at == slots - 1 else at // 2 * 2 + (parity if at % 2 == 0 else 1 - parity)
        copies.append(pltpu.make_async_copy(key_refs[at], key_all.at[slot], sems.at[2 * at]))
        copies.append(
            pltpu.make_async_copy(value_refs[at], value_all.at[slot], sems.at[2 * at + 1])
        )

    def fetch():
        for copy in copies:
            copy.start()

    def wait():
        for copy in copies:
            copy.wait()

    if resume:
        fetch()
        sub_row = local_row // SUB
        state_copies = [
            pltpu.make_async_copy(
                state.at[pl.ds(sub_row, subs)], ref, sems.at[2 * slots + 1 + at]
            )
            for at, (state, ref) in enumerate(zip(states, (acc, peak, total)))
        ]
        for copy in state_copies:
            copy.start()
        out_cols = w_buf.shape[2]
        w_copies = []
        for at in range(4):
            column = pl.multiple_of(place[5 + at] * out_cols, out_cols)
            w_copies.append(
                pltpu.make_async_copy(
                    w_ref.at[:, pl.ds(column, out_cols)], w_buf.at[at], w_sems.at[at]
                )
            )
        for copy in w_copies:
            copy.start()
    else:
        pl.when(step_id == 0)(fetch)

    last_row = first_row + rows - 1
    one_head = [
        first_row + sub * SUB + lax.broadcasted_iota(jnp.int32, (1, SUB), 1) for sub in range(subs)
    ]
    begin = [jnp.zeros((1, SUB), jnp.int32)] * subs
    begin_first = jnp.int32(0)
    begin_last = jnp.int32(0)
    start = jnp.int32(0)
    for doc in range(lengths.shape[0]):
        begin = [
            jnp.where(one >= start, jnp.maximum(old, start), old)
            for one, old in zip(one_head, begin)
        ]
        begin_first = jnp.where(first_row >= start, jnp.maximum(begin_first, start), begin_first)
        begin_last = jnp.where(last_row >= start, jnp.maximum(begin_last, start), begin_last)
        start = start + lengths[doc]

    task = (first_row // q_block) * heads
    lows = [tasks[(task + head) * 5 + 2] * q_block for head in range(heads)]
    highs = [tasks[(task + head) * 5 + 3] * q_block for head in range(heads)]
    low_least, low_most, high_least, high_most = lows[0], lows[0], highs[0], highs[0]
    for low, high in zip(lows[1:], highs[1:]):
        low_least, low_most = jnp.minimum(low_least, low), jnp.maximum(low_most, low)
        high_least, high_most = jnp.minimum(high_least, high), jnp.maximum(high_most, high)
    begins, ends = [], []
    for sub in range(subs):
        for group in range(groups):
            members = range(group * PAIR, (group + 1) * PAIR)
            begins.append(
                jnp.concatenate([jnp.maximum(begin[sub], lows[m]) for m in members], axis=1)
            )
            ends.append(
                jnp.concatenate([jnp.minimum(one_head[sub], highs[m] - 1) for m in members], axis=1)
            )

    ratio = key_tile // edge_tile
    tiles = limit // edge_tile
    lo = jnp.clip((jnp.maximum(low_least, begin_first) - base) // edge_tile, 0, tiles)
    hi = jnp.clip(
        (jnp.minimum(high_most, last_row + 1) - base + edge_tile - 1) // edge_tile, lo, tiles
    )
    full_lo = (jnp.maximum(low_most, begin_last) - base + key_tile - 1) // key_tile
    full_hi = (jnp.minimum(high_least, first_row + 1) - base) // key_tile
    full_lo = jnp.maximum(full_lo, 0)
    full_hi = jnp.minimum(full_hi, tiles // ratio)
    some = full_hi > full_lo
    inner_lo = jnp.where(some, full_lo * ratio, lo)
    inner_hi = jnp.where(some, full_hi * ratio, lo)
    factor = math.log2(math.e) / math.sqrt(width)

    if resume:
        for copy in state_copies:
            copy.wait()
        wait()
    else:
        acc[...] = jnp.zeros_like(acc)
        peak[...] = jnp.full_like(peak, FLOOR_SCORE)
        total[...] = jnp.zeros_like(total)
        pl.when(step_id == 0)(wait)
    q_copy.wait()

    def sweep(count, tile_of, size, masked, fixed):
        per_shard = shard_rows // size

        def keys_of(tile):
            offset = pl.multiple_of((tile % per_shard) * size, size)
            return key_all[tile // per_shard, pl.ds(offset, size), :]

        def values_of(tile):
            offset = pl.multiple_of((tile % per_shard) * size, size)
            values = value_all[tile // per_shard, :, pl.ds(offset, size)]
            return jnp.concatenate([values, jnp.ones((16, size), jnp.bfloat16)], axis=0)

        def scores_of(keys, unit):
            sub, group = divmod(unit, groups)
            asked = q_buf[group * PAIR : (group + 1) * PAIR, sub * SUB : (sub + 1) * SUB, :]
            return lax.dot_general(
                keys,
                asked.reshape(cols, width),
                (((1,), (1,)), ((), ())),
                preferred_element_type=jnp.float32,
            )

        def gather(values, unit, weights, rescale):
            at = divmod(unit, groups)
            product = lax.dot_general(
                values, weights, (((1,), (0,)), ((), ())), preferred_element_type=jnp.float32
            )
            if fixed:
                total[at] += product[width : width + 1]
                acc[at] += product[:width]
            else:
                total[at] = total[at] * rescale + product[width : width + 1]
                acc[at] = acc[at] * rescale + product[:width]

        def step(turn, carried):
            tile = tile_of(turn)
            keys, values = keys_of(tile), values_of(tile)
            key_pos = (
                base + tile * size + lax.broadcasted_iota(jnp.int32, (size, 1), 0)
                if masked
                else None
            )
            scores = s_buf[:size]
            waiting = None
            for unit in range(units):
                at = divmod(unit, groups)
                if unit + 1 < units:
                    ahead = scores_of(keys, unit + 1)
                else:
                    ahead = scores_of(keys_of(tile_of(jnp.minimum(turn + 1, count - 1))), 0)
                if masked:
                    visible = (key_pos >= begins[unit]) & (key_pos <= ends[unit])
                    scores = jnp.where(visible, scores, FLOOR_SCORE)
                before = peak[at]
                if fixed:
                    now, rescale = before, None
                else:
                    now = jnp.maximum(before, jnp.max(scores, axis=0, keepdims=True) * factor)
                    peak[at] = now
                    rescale = jnp.exp2(before - now)
                weights = jnp.exp2(scores * factor - now).astype(jnp.bfloat16)
                if waiting is not None:
                    gather(values, unit - 1, *waiting)
                else:
                    earlier = values_of(tile_of(jnp.maximum(turn - 1, 0)))
                    gather(earlier, units - 1, p_buf[:size], rescale_buf[...])
                waiting = weights, rescale
                scores = ahead
            s_buf[:size] = scores
            p_buf[:size] = waiting[0]
            if not fixed:
                rescale_buf[...] = waiting[1]
            return carried

        def whole():
            p_buf[:size] = jnp.zeros((size, cols), jnp.bfloat16)
            rescale_buf[...] = jnp.ones_like(rescale_buf)
            s_buf[:size] = scores_of(keys_of(tile_of(0)), 0)
            lax.fori_loop(0, count, step, 0)
            gather(values_of(tile_of(count - 1)), units - 1, p_buf[:size], rescale_buf[...])

        pl.when(count > 0)(whole)

    sweep(
        (inner_hi - inner_lo) // ratio,
        lambda turn: inner_lo // ratio + turn,
        key_tile,
        False,
        resume,
    )
    left = inner_lo - lo
    sweep(
        left + hi - inner_hi,
        lambda turn: jnp.where(turn < left, lo + turn, inner_hi + turn - left),
        edge_tile,
        True,
        resume,
    )
    if not resume:
        outs[0][...] = acc[...]
        outs[1][...] = peak[...]
        outs[2][...] = total[...]
        return
    in_range = jnp.min(jnp.where(total[...] < SAFE_TOTAL, 1.0, 0.0))

    @pl.when(in_range < 0.5)
    def again():
        for copy in state_copies:
            copy.start()
        for copy in state_copies:
            copy.wait()
        sweep(hi - lo, lambda turn: lo + turn, edge_tile, True, False)

    for sub in range(subs):
        for group in range(groups):
            done = (acc[sub, group] / total[sub, group]).T.astype(jnp.bfloat16)
            for member in range(PAIR):
                head = group * PAIR + member
                attended[sub * SUB : (sub + 1) * SUB, head * width : (head + 1) * width] = done[
                    member * SUB : (member + 1) * SUB
                ]
    for at in range(4):
        w_copies[at].wait()
        product = jnp.dot(attended[...], w_buf[at], preferred_element_type=jnp.float32)
        ref = sent_ref if at < 2 else kept_ref
        column = (at % 2) * out_cols
        ref[:, column : column + out_cols] = product.astype(ref.dtype)


def attend(place, lengths, tasks, queries, kvs, subs, q_block, states=None, w_out=None, out_cols=0):
    heads, tok_dev, width = queries.shape
    shard_rows = kvs[0][0].shape[0]
    slots = len(kvs)
    key_tile = min(KEY_TILE, shard_rows)
    edge_tile = min(EDGE_TILE, key_tile)
    resume = states is not None
    groups, cols, rows = heads // PAIR, PAIR * SUB, subs * SUB
    state_shapes = [(groups, width, cols), (groups, 1, cols), (groups, 1, cols)]
    hbm = pl.BlockSpec(memory_space=pl.ANY)
    scratch = [
        pltpu.VMEM((heads, rows, width), jnp.bfloat16),
        pltpu.VMEM((slots, shard_rows, width), jnp.bfloat16),
        pltpu.VMEM((slots, width, shard_rows), jnp.bfloat16),
        *[pltpu.VMEM((subs,) + shape, jnp.float32) for shape in state_shapes],
        pltpu.VMEM((key_tile, cols), jnp.float32),
        pltpu.VMEM((key_tile, cols), jnp.bfloat16),
        pltpu.VMEM((1, cols), jnp.float32),
        pltpu.SemaphoreType.DMA((2 * slots + 4,)),
    ]
    if resume:
        extra = [*states, w_out]
        out_specs = [pl.BlockSpec((rows, 2 * out_cols), lambda i, *_: (0, 0))] * 2
        out_shape = [
            jax.ShapeDtypeStruct((rows, 2 * out_cols), jnp.bfloat16),
            jax.ShapeDtypeStruct((rows, 2 * out_cols), jnp.float32),
        ]
        scratch += [
            pltpu.VMEM((4, heads * width, out_cols), jnp.bfloat16),
            pltpu.VMEM((rows, heads * width), jnp.bfloat16),
            pltpu.SemaphoreType.DMA((4,)),
        ]
    else:
        extra = []
        out_specs = [
            pl.BlockSpec((subs,) + shape, lambda i, *_: (i, 0, 0, 0)) for shape in state_shapes
        ]
        out_shape = [
            jax.ShapeDtypeStruct((tok_dev // SUB,) + shape, jnp.float32) for shape in state_shapes
        ]
    return pl.pallas_call(
        partial(
            attend_kernel,
            slots=slots,
            subs=subs,
            q_block=q_block,
            key_tile=key_tile,
            edge_tile=edge_tile,
            resume=resume,
        ),
        grid_spec=pltpu.PrefetchScalarGridSpec(
            num_scalar_prefetch=3,
            grid=(1 if resume else tok_dev // rows,),
            in_specs=[hbm] * (1 + 2 * slots + len(extra)),
            out_specs=out_specs,
            scratch_shapes=scratch,
        ),
        out_shape=out_shape,
        compiler_params=pltpu.CompilerParams(vmem_limit_bytes=40 * 2**20),
        cost_estimate=pl.CostEstimate(
            flops=heads * rows * 4096 * width * 4,
            bytes_accessed=8 * 2**20,
            transcendentals=heads * rows * 4096,
        ),
    )(place, lengths, tasks, queries, *[k for k, _ in kvs], *[v for _, v in kvs], *extra)


def local(queries, keys, values, doc_lengths, tasks, w_out):
    heads, tok_dev, width = queries.shape
    n_tok = lax.axis_size("tok")
    n_head = lax.axis_size("head")
    me = lax.axis_index("tok")
    z = lax.axis_index("head")
    tokens = n_tok * tok_dev
    q_block = tokens * heads // tasks.shape[0]
    chips = n_tok // 2
    doc_most = tokens * 4 // doc_lengths.shape[0]
    back = min(chips - 1, -(-(doc_most - 1) // (2 * tok_dev)))
    out_cols = w_out.shape[1] // n_head
    flat_tasks = tasks.reshape(-1)

    own = keys[0], values[0].T
    spans = []
    for hop in range(back, 0, -1):
        pairs = [(i, i + 2 * hop) for i in range(n_tok - 2 * hop)]
        spans.append(tuple(lax.ppermute(part, "tok", pairs) for part in own))
    swap = [(i, i ^ 1) for i in range(n_tok)]

    columns = [(z ^ 1) ^ 2, z ^ 1, z ^ 2, z]

    def placed(base, limit, row):
        numbers = [me % 2, me * tok_dev + row, base, limit, row, *columns]
        return jnp.stack([jnp.asarray(n, jnp.int32) for n in numbers])

    states = attend(
        placed(me * tok_dev, tok_dev, 0),
        doc_lengths,
        flat_tasks,
        queries,
        [own],
        tok_dev // SUB // FIRST_PARTS,
        q_block,
    )
    spans, states = lax.optimization_barrier((spans, states))
    kvs = []
    for mine in spans:
        kvs += [mine, tuple(lax.ppermute(part, "tok", swap) for part in mine)]
    kvs.append(tuple(lax.ppermute(part, "tok", swap) for part in own))
    base = (me // 2 - back) * 2 * tok_dev

    near = [(i, i ^ 1) for i in range(n_head)]
    far = [(i, i ^ 2) for i in range(n_head)]

    def hop(kept, arrived):
        summed = kept + arrived.astype(jnp.float32)
        return summed[:, :out_cols].astype(jnp.bfloat16), summed[:, out_cols:]

    halves = []
    kept = sent = summed = None
    row = 0
    for part in PARTS:
        subs = tok_dev // SUB * part // sum(PARTS)
        place = placed(base, me * tok_dev - base, row)
        row += subs * SUB
        place, sent, summed = lax.optimization_barrier((place, sent, summed))
        arrived = None if sent is None else lax.ppermute(sent, "head", near)
        crossed = None if summed is None else lax.ppermute(summed[0], "head", far)
        sent, kept_now = attend(
            place, doc_lengths, flat_tasks, queries, kvs, subs, q_block, states, w_out, out_cols
        )
        sent, arrived, crossed = lax.optimization_barrier((sent, arrived, crossed))
        if crossed is not None:
            halves.append((summed[1], crossed))
        summed = None if arrived is None else hop(kept, arrived)
        kept = kept_now
    arrived = lax.ppermute(sent, "head", near)
    if summed is not None:
        halves.append((summed[1], lax.ppermute(summed[0], "head", far)))
    summed = hop(kept, arrived)
    halves.append((summed[1], lax.ppermute(summed[0], "head", far)))
    outs = [(held + crossed.astype(jnp.float32)).astype(jnp.bfloat16) for held, crossed in halves]
    return jnp.concatenate(outs, axis=0)


def solution(mesh):
    placed = (
        P("head", "tok", None),
        P("head", "tok", None),
        P("head", "tok", None),
        P(),
        P(),
        P("head", None),
    )
    return jax.shard_map(
        local, mesh=mesh, in_specs=placed, out_specs=P("tok", "head"), check_vma=False
    )
```

```python
from functools import partial
import math

import jax
import jax.numpy as jnp
from jax import lax
from jax.experimental import pallas as pl
from jax.experimental.pallas import tpu as pltpu
from jax.sharding import PartitionSpec as P

FLOOR_SCORE = -1e30
SAFE_TOTAL = 2.0**100
KEY_TILE = 512
EDGE_TILE = 256
VMEM_BYTES = 60 * 2**20
SUB = 128
PAIR = 4
FIRST_PARTS = 4
PARTS = (2, 2, 2, 2)


def attend_kernel(
    place, lengths, tasks, q_ref, *refs, slots, subs, q_block, key_tile, edge_tile, resume
):
    kv_refs, refs = refs[:slots], refs[slots:]
    if resume:
        states, w_ref, refs = refs[:3], refs[3], refs[4:]
        sent_ref, pass_ref, keep_ref, q_buf, kv_all, acc, peak, total = refs[:8]
        s_buf, p_buf, v_buf, rescale_buf, sems, w_buf, attended, w_sems = refs[8:]
    else:
        outs, refs = refs[:3], refs[3:]
        q_buf, kv_all, acc, peak, total, s_buf, p_buf, v_buf, rescale_buf, sems = refs
    heads, _, width = q_ref.shape
    shard_rows = kv_refs[0].shape[1]
    groups = heads // PAIR
    units = subs * groups
    cols = PAIR * SUB
    rows = subs * SUB
    step_id = pl.program_id(0)
    parity = place[0]
    first_row = place[1] + step_id * rows
    base = place[2]
    limit = place[3]
    local_row = place[4] + step_id * rows

    q_copy = pltpu.make_async_copy(
        q_ref.at[:, pl.ds(pl.multiple_of(local_row, SUB), rows), :], q_buf, sems.at[slots]
    )
    q_copy.start()
    copies = []
    for at in range(slots):
        slot = at if at == slots - 1 else at // 2 * 2 + (parity if at % 2 == 0 else 1 - parity)
        copies.append(pltpu.make_async_copy(kv_refs[at], kv_all.at[slot], sems.at[at]))

    def fetch():
        for copy in copies:
            copy.start()

    def wait():
        for copy in copies:
            copy.wait()

    if resume:
        fetch()
        sub_row = local_row // SUB
        state_copies = [
            pltpu.make_async_copy(
                state.at[pl.ds(sub_row, subs)], ref, sems.at[slots + 1 + at]
            )
            for at, (state, ref) in enumerate(zip(states, (acc, peak, total)))
        ]
        for copy in state_copies:
            copy.start()
        out_cols = w_buf.shape[2]
        w_copies = []
        for at in range(4):
            column = pl.multiple_of(place[5 + at] * out_cols, out_cols)
            w_copies.append(
                pltpu.make_async_copy(
                    w_ref.at[:, pl.ds(column, out_cols)], w_buf.at[at], w_sems.at[at]
                )
            )
    else:
        pl.when(step_id == 0)(fetch)

    last_row = first_row + rows - 1
    one_head = [
        first_row + sub * SUB + lax.broadcasted_iota(jnp.int32, (1, SUB), 1) for sub in range(subs)
    ]
    begin = [jnp.zeros((1, SUB), jnp.int32)] * subs
    begin_first = jnp.int32(0)
    begin_last = jnp.int32(0)
    start = jnp.int32(0)
    for doc in range(lengths.shape[0]):
        begin = [
            jnp.where(one >= start, jnp.maximum(old, start), old)
            for one, old in zip(one_head, begin)
        ]
        begin_first = jnp.where(first_row >= start, jnp.maximum(begin_first, start), begin_first)
        begin_last = jnp.where(last_row >= start, jnp.maximum(begin_last, start), begin_last)
        start = start + lengths[doc]

    task = (first_row // q_block) * heads
    lows = [tasks[(task + head) * 5 + 2] * q_block for head in range(heads)]
    highs = [tasks[(task + head) * 5 + 3] * q_block for head in range(heads)]
    low_least, low_most, high_least, high_most = lows[0], lows[0], highs[0], highs[0]
    for low, high in zip(lows[1:], highs[1:]):
        low_least, low_most = jnp.minimum(low_least, low), jnp.maximum(low_most, low)
        high_least, high_most = jnp.minimum(high_least, high), jnp.maximum(high_most, high)
    begins, ends = [], []
    for sub in range(subs):
        for group in range(groups):
            members = range(group * PAIR, (group + 1) * PAIR)
            begins.append(
                jnp.concatenate([jnp.maximum(begin[sub], lows[m]) for m in members], axis=1)
            )
            ends.append(
                jnp.concatenate([jnp.minimum(one_head[sub], highs[m] - 1) for m in members], axis=1)
            )

    ratio = key_tile // edge_tile
    tiles = limit // edge_tile
    lo = jnp.clip((jnp.maximum(low_least, begin_first) - base) // edge_tile, 0, tiles)
    hi = jnp.clip(
        (jnp.minimum(high_most, last_row + 1) - base + edge_tile - 1) // edge_tile, lo, tiles
    )
    full_lo = (jnp.maximum(low_most, begin_last) - base + key_tile - 1) // key_tile
    full_hi = (jnp.minimum(high_least, first_row + 1) - base) // key_tile
    full_lo = jnp.maximum(full_lo, 0)
    full_hi = jnp.minimum(full_hi, tiles // ratio)
    some = full_hi > full_lo
    inner_lo = jnp.where(some, full_lo * ratio, lo)
    inner_hi = jnp.where(some, full_hi * ratio, lo)
    factor = math.log2(math.e) / math.sqrt(width)

    if resume:
        for copy in state_copies:
            copy.wait()
        wait()
        for copy in w_copies:
            copy.start()
    else:
        acc[...] = jnp.zeros_like(acc)
        peak[...] = jnp.full_like(peak, FLOOR_SCORE)
        total[...] = jnp.zeros_like(total)
        pl.when(step_id == 0)(wait)
    q_copy.wait()

    def sweep(count, tile_of, size, masked, fixed):
        per_shard = shard_rows // size

        def keys_of(tile):
            offset = pl.multiple_of((tile % per_shard) * size, size)
            return kv_all[tile // per_shard, 0, pl.ds(offset, size), :]

        def values_of(tile):
            offset = pl.multiple_of((tile % per_shard) * size, size)
            values = kv_all[tile // per_shard, 1, pl.ds(offset, size), :].T
            return jnp.concatenate([values, jnp.ones((16, size), jnp.bfloat16)], axis=0)

        def scores_of(keys, unit):
            sub, group = divmod(unit, groups)
            asked = q_buf[group * PAIR : (group + 1) * PAIR, sub * SUB : (sub + 1) * SUB, :]
            return lax.dot_general(
                keys,
                asked.reshape(cols, width),
                (((1,), (1,)), ((), ())),
                preferred_element_type=jnp.float32,
            )

        def gather(values, unit, weights, rescale):
            at = divmod(unit, groups)
            product = lax.dot_general(
                values, weights, (((1,), (0,)), ((), ())), preferred_element_type=jnp.float32
            )
            if fixed:
                total[at] += product[width : width + 1]
                acc[at] += product[:width]
            else:
                total[at] = total[at] * rescale + product[width : width + 1]
                acc[at] = acc[at] * rescale + product[:width]

        def step(turn, carried):
            tile = tile_of(turn)
            keys, values = keys_of(tile), values_of(tile)
            key_pos = (
                base + tile * size + lax.broadcasted_iota(jnp.int32, (size, 1), 0)
                if masked
                else None
            )
            scores = s_buf[:size]
            waiting = None
            for unit in range(units):
                at = divmod(unit, groups)
                if unit + 1 < units:
                    ahead = scores_of(keys, unit + 1)
                else:
                    ahead = scores_of(keys_of(tile_of(jnp.minimum(turn + 1, count - 1))), 0)
                if masked:
                    visible = (key_pos >= begins[unit]) & (key_pos <= ends[unit])
                    scores = jnp.where(visible, scores, FLOOR_SCORE)
                before = peak[at]
                if fixed:
                    now, rescale = before, None
                else:
                    now = jnp.maximum(before, jnp.max(scores, axis=0, keepdims=True) * factor)
                    peak[at] = now
                    rescale = jnp.exp2(before - now)
                weights = jnp.exp2(scores * factor - now).astype(jnp.bfloat16)
                if waiting is not None:
                    gather(values, unit - 1, *waiting)
                else:
                    gather(v_buf[:, :size], units - 1, p_buf[:size], rescale_buf[...])
                waiting = weights, rescale
                scores = ahead
            s_buf[:size] = scores
            v_buf[:, :size] = values
            p_buf[:size] = waiting[0]
            if not fixed:
                rescale_buf[...] = waiting[1]
            return carried

        def whole():
            p_buf[:size] = jnp.zeros((size, cols), jnp.bfloat16)
            rescale_buf[...] = jnp.ones_like(rescale_buf)
            v_buf[:, :size] = jnp.zeros((width + 16, size), jnp.bfloat16)
            s_buf[:size] = scores_of(keys_of(tile_of(0)), 0)
            lax.fori_loop(0, count, step, 0)
            gather(v_buf[:, :size], units - 1, p_buf[:size], rescale_buf[...])

        pl.when(count > 0)(whole)

    sweep(
        (inner_hi - inner_lo) // ratio,
        lambda turn: inner_lo // ratio + turn,
        key_tile,
        False,
        resume,
    )
    left = inner_lo - lo
    sweep(
        left + hi - inner_hi,
        lambda turn: jnp.where(turn < left, lo + turn, inner_hi + turn - left),
        edge_tile,
        True,
        resume,
    )
    if not resume:
        outs[0][...] = acc[...]
        outs[1][...] = peak[...]
        outs[2][...] = total[...]
        return
    in_range = jnp.min(jnp.where(total[...] < SAFE_TOTAL, 1.0, 0.0))

    @pl.when(in_range < 0.5)
    def again():
        for copy in state_copies:
            copy.start()
        for copy in state_copies:
            copy.wait()
        sweep(hi - lo, lambda turn: lo + turn, edge_tile, True, False)

    for sub in range(subs):
        for group in range(groups):
            done = (acc[sub, group] / total[sub, group]).T.astype(jnp.bfloat16)
            for member in range(PAIR):
                head = group * PAIR + member
                attended[sub * SUB : (sub + 1) * SUB, head * width : (head + 1) * width] = done[
                    member * SUB : (member + 1) * SUB
                ]
    for at in range(4):
        w_copies[at].wait()
        product = jnp.dot(attended[...], w_buf[at], preferred_element_type=jnp.float32)
        if at < 2:
            sent_ref[:, at * out_cols : (at + 1) * out_cols] = product.astype(jnp.bfloat16)
        elif at == 2:
            pass_ref[...] = product
        else:
            keep_ref[...] = product


def attend(place, lengths, tasks, queries, kvs, subs, q_block, states=None, w_out=None, out_cols=0):
    heads, tok_dev, width = queries.shape
    shard_rows = kvs[0].shape[1]
    slots = len(kvs)
    key_tile = min(KEY_TILE, shard_rows)
    edge_tile = min(EDGE_TILE, key_tile)
    resume = states is not None
    groups, cols, rows = heads // PAIR, PAIR * SUB, subs * SUB
    state_shapes = [(groups, width, cols), (groups, 1, cols), (groups, 1, cols)]
    hbm = pl.BlockSpec(memory_space=pltpu.HBM)
    scratch = [
        pltpu.VMEM((heads, rows, width), jnp.bfloat16),
        pltpu.VMEM((slots, 2, shard_rows, width), jnp.bfloat16),
        *[pltpu.VMEM((subs,) + shape, jnp.float32) for shape in state_shapes],
        pltpu.VMEM((key_tile, cols), jnp.float32),
        pltpu.VMEM((key_tile, cols), jnp.bfloat16),
        pltpu.VMEM((width + 16, key_tile), jnp.bfloat16),
        pltpu.VMEM((1, cols), jnp.float32),
        pltpu.SemaphoreType.DMA((slots + 4,)),
    ]
    if resume:
        extra = [*states, w_out]
        out_specs = [pl.BlockSpec((rows, n * out_cols), lambda i, *_: (0, 0)) for n in (2, 1, 1)]
        out_shape = [
            jax.ShapeDtypeStruct((rows, 2 * out_cols), jnp.bfloat16),
            jax.ShapeDtypeStruct((rows, out_cols), jnp.float32),
            jax.ShapeDtypeStruct((rows, out_cols), jnp.float32),
        ]
        scratch += [
            pltpu.VMEM((4, heads * width, out_cols), jnp.bfloat16),
            pltpu.VMEM((rows, heads * width), jnp.bfloat16),
            pltpu.SemaphoreType.DMA((4,)),
        ]
    else:
        extra = []
        out_specs = [
            pl.BlockSpec((subs,) + shape, lambda i, *_: (i, 0, 0, 0)) for shape in state_shapes
        ]
        out_shape = [
            jax.ShapeDtypeStruct((tok_dev // SUB,) + shape, jnp.float32) for shape in state_shapes
        ]
    return pl.pallas_call(
        partial(
            attend_kernel,
            slots=slots,
            subs=subs,
            q_block=q_block,
            key_tile=key_tile,
            edge_tile=edge_tile,
            resume=resume,
        ),
        grid_spec=pltpu.PrefetchScalarGridSpec(
            num_scalar_prefetch=3,
            grid=(1 if resume else tok_dev // rows,),
            in_specs=[hbm] * (1 + slots + len(extra)),
            out_specs=out_specs,
            scratch_shapes=scratch,
        ),
        out_shape=out_shape,
        compiler_params=pltpu.CompilerParams(vmem_limit_bytes=VMEM_BYTES),
        cost_estimate=pl.CostEstimate(
            flops=heads * rows * 4096 * width * 4,
            bytes_accessed=8 * 2**20,
            transcendentals=heads * rows * 4096,
        ),
    )(place, lengths, tasks, queries, *kvs, *extra)


def local(queries, keys, values, doc_lengths, tasks, w_out):
    heads, tok_dev, width = queries.shape
    n_tok = lax.axis_size("tok")
    n_head = lax.axis_size("head")
    me = lax.axis_index("tok")
    z = lax.axis_index("head")
    tokens = n_tok * tok_dev
    q_block = tokens * heads // tasks.shape[0]
    chips = n_tok // 2
    doc_most = tokens * 4 // doc_lengths.shape[0]
    back = min(chips - 1, -(-(doc_most - 1) // (2 * tok_dev)))
    out_cols = w_out.shape[1] // n_head
    flat_tasks = tasks.reshape(-1)

    own = jnp.concatenate([keys, values], axis=0)
    spans = []
    for hop in range(back, 0, -1):
        pairs = [(i, i + 2 * hop) for i in range(n_tok - 2 * hop)]
        spans.append(lax.ppermute(own, "tok", pairs))
    swap = [(i, i ^ 1) for i in range(n_tok)]

    columns = [(z ^ 1) ^ 2, z ^ 1, z ^ 2, z]

    def placed(base, limit, row):
        numbers = [me % 2, me * tok_dev + row, base, limit, row, *columns]
        return jnp.stack([jnp.asarray(n, jnp.int32) for n in numbers])

    states = attend(
        placed(me * tok_dev, tok_dev, 0),
        doc_lengths,
        flat_tasks,
        queries,
        [own],
        tok_dev // SUB // FIRST_PARTS,
        q_block,
    )
    spans, states = lax.optimization_barrier((spans, states))
    kvs = []
    for mine in spans:
        kvs += [mine, lax.ppermute(mine, "tok", swap)]
    kvs.append(lax.ppermute(own, "tok", swap))
    base = (me // 2 - back) * 2 * tok_dev

    near = [(i, i ^ 1) for i in range(n_head)]
    far = [(i, i ^ 2) for i in range(n_head)]

    def onward(passed, arrived):
        return (passed + arrived[:, :out_cols].astype(jnp.float32)).astype(jnp.bfloat16)

    terms = []
    sent = passed = kept = other = held = None
    row = 0
    for part in PARTS:
        subs = tok_dev // SUB * part // sum(PARTS)
        place = placed(base, me * tok_dev - base, row)
        row += subs * SUB
        place, sent, other = lax.optimization_barrier((place, sent, other))
        arrived = None if sent is None else lax.ppermute(sent, "head", near)
        crossed = None if other is None else lax.ppermute(other, "head", far)
        sent, passed_now, kept_now = attend(
            place, doc_lengths, flat_tasks, queries, kvs, subs, q_block, states, w_out, out_cols
        )
        sent, arrived, crossed = lax.optimization_barrier((sent, arrived, crossed))
        if crossed is not None:
            terms.append((*held, crossed))
        if arrived is not None:
            other, held = onward(passed, arrived), (kept, arrived)
        passed, kept = passed_now, kept_now
    arrived = lax.ppermute(sent, "head", near)
    if other is not None:
        terms.append((*held, lax.ppermute(other, "head", far)))
    terms.append((kept, arrived, lax.ppermute(onward(passed, arrived), "head", far)))
    outs = [
        (kept + arrived[:, out_cols:].astype(jnp.float32) + crossed.astype(jnp.float32)).astype(
            jnp.bfloat16
        )
        for kept, arrived, crossed in terms
    ]
    return jnp.concatenate(outs, axis=0)


def solution(mesh):
    placed = (
        P("head", "tok", None),
        P("head", "tok", None),
        P("head", "tok", None),
        P(),
        P(),
        P("head", None),
    )
    return jax.shard_map(
        local, mesh=mesh, in_specs=placed, out_specs=P("tok", "head"), check_vma=False
    )
```

```python
from functools import partial
import math

import jax
import jax.numpy as jnp
from jax import lax
from jax.experimental import pallas as pl
from jax.experimental.pallas import tpu as pltpu
from jax.sharding import PartitionSpec as P

FLOOR_SCORE = -1e30
SAFE_TOTAL = 2.0**100
KEY_TILE = 512
EDGE_TILE = 256
VMEM_BYTES = 40 * 2**20
SUB = 128
LAG = 2
PAIR = 4
PARTS = (1, 2, 2, 2, 1)


def attend_kernel(place, lengths, tasks, q_ref, *refs, slots, subs, q_block, key_tile, edge_tile):
    kv_refs, refs = refs[:slots], refs[slots:]
    out_ref, q_buf, kv_all, acc, peak, total, s_buf, p_buf, rescale_buf, sems = refs
    heads, _, width = q_ref.shape
    shard_rows = kv_refs[0].shape[1]
    groups = heads // PAIR
    units = subs * groups
    cols = PAIR * SUB
    rows = subs * SUB
    parity = place[0]
    first_row = place[1]
    base = place[2]
    q_copy = pltpu.make_async_copy(
        q_ref.at[:, pl.ds(pl.multiple_of(place[3], SUB), rows), :], q_buf, sems.at[slots]
    )
    q_copy.start()

    last_row = first_row + rows - 1
    one_head = [
        first_row + sub * SUB + lax.broadcasted_iota(jnp.int32, (1, SUB), 1) for sub in range(subs)
    ]
    begin = [jnp.zeros((1, SUB), jnp.int32)] * subs
    begin_first = jnp.int32(0)
    begin_last = jnp.int32(0)
    start = jnp.int32(0)
    for doc in range(lengths.shape[0]):
        begin = [
            jnp.where(one >= start, jnp.maximum(old, start), old)
            for one, old in zip(one_head, begin)
        ]
        begin_first = jnp.where(first_row >= start, jnp.maximum(begin_first, start), begin_first)
        begin_last = jnp.where(last_row >= start, jnp.maximum(begin_last, start), begin_last)
        start = start + lengths[doc]

    begins, ends, lows, highs = [], [], [], []
    for sub in range(subs):
        task = ((first_row + sub * SUB) // q_block) * heads
        low = [tasks[(task + head) * 5 + 2] * q_block for head in range(heads)]
        high = [tasks[(task + head) * 5 + 3] * q_block for head in range(heads)]
        for group in range(groups):
            members = range(group * PAIR, (group + 1) * PAIR)
            begins.append(
                jnp.concatenate([jnp.maximum(begin[sub], low[m]) for m in members], axis=1)
            )
            ends.append(
                jnp.concatenate([jnp.minimum(one_head[sub], high[m] - 1) for m in members], axis=1)
            )
        lows += low
        highs += high
    low_least, low_most, high_least, high_most = lows[0], lows[0], highs[0], highs[0]
    for low, high in zip(lows[1:], highs[1:]):
        low_least, low_most = jnp.minimum(low_least, low), jnp.maximum(low_most, low)
        high_least, high_most = jnp.minimum(high_least, high), jnp.maximum(high_most, high)

    ratio = key_tile // edge_tile
    tiles = slots * shard_rows // edge_tile
    lo = jnp.clip((jnp.maximum(low_least, begin_first) - base) // edge_tile, 0, tiles)
    hi = jnp.clip(
        (jnp.minimum(high_most, last_row + 1) - base + edge_tile - 1) // edge_tile, lo, tiles
    )
    full_lo = (jnp.maximum(low_most, begin_last) - base + key_tile - 1) // key_tile
    full_hi = (jnp.minimum(high_least, first_row + 1) - base) // key_tile
    full_lo = jnp.maximum(full_lo, 0)
    full_hi = jnp.minimum(full_hi, tiles // ratio)
    some = full_hi > full_lo
    inner_lo = jnp.where(some, full_lo * ratio, lo)
    inner_hi = jnp.where(some, full_hi * ratio, lo)
    factor = math.log2(math.e) / math.sqrt(width)

    def reset():
        acc[...] = jnp.zeros_like(acc)
        peak[...] = jnp.full_like(peak, FLOOR_SCORE)
        total[...] = jnp.zeros_like(total)

    per_slot = shard_rows // edge_tile
    early, late = [], []
    for at in range(slots):
        slot = at // 2 * 2 + (parity if at % 2 == 0 else 1 - parity)
        copy = pltpu.make_async_copy(kv_refs[at], kv_all.at[slot], sems.at[at])
        first, last = slot * per_slot, (slot + 1) * per_slot
        below = (lo < inner_lo) & (lo < last) & (inner_lo > first)
        above = (inner_hi < hi) & (inner_hi < last) & (hi > first)
        used = (lo < last) & (hi > first)
        early.append((below | above, copy))
        late.append((used & jnp.logical_not(below | above), copy))
    for needed, copy in early + late:
        pl.when(needed)(copy.start)

    def wait(copies):
        for needed, copy in copies:
            pl.when(needed)(copy.wait)

    reset()
    q_copy.wait()
    wait(early)

    def sweep(count, tile_of, size, masked, fixed):
        per_shard = shard_rows // size

        def keys_of(tile):
            offset = pl.multiple_of((tile % per_shard) * size, size)
            return kv_all[tile // per_shard, 0, pl.ds(offset, size), :]

        def values_of(tile):
            offset = pl.multiple_of((tile % per_shard) * size, size)
            values = kv_all[tile // per_shard, 1, pl.ds(offset, size), :]
            values = [values[at : at + width] for at in range(0, size, width)]
            values = jnp.concatenate(values, axis=1)
            return jnp.concatenate([values, jnp.ones((16, size), jnp.bfloat16)], axis=0)

        def scores_of(keys, unit):
            sub, group = divmod(unit, groups)
            asked = q_buf[group * PAIR : (group + 1) * PAIR, sub * SUB : (sub + 1) * SUB, :]
            return lax.dot_general(
                keys,
                asked.reshape(cols, width),
                (((1,), (1,)), ((), ())),
                preferred_element_type=jnp.float32,
            )

        def gather(values, unit, weights, rescale):
            at = divmod(unit, groups)
            product = lax.dot_general(
                values, weights, (((1,), (0,)), ((), ())), preferred_element_type=jnp.float32
            )
            if fixed:
                total[at] += product[width : width + 1]
                acc[at] += product[:width]
            else:
                total[at] = total[at] * rescale + product[width : width + 1]
                acc[at] = acc[at] * rescale + product[:width]

        def step(turn, carried):
            tile = tile_of(turn)
            keys, values = keys_of(tile), values_of(tile)
            key_pos = (
                base + tile * size + lax.broadcasted_iota(jnp.int32, (size, 1), 0)
                if masked
                else None
            )
            scores = s_buf[:size]
            waiting = None
            for unit in range(units):
                at = divmod(unit, groups)
                if unit + 1 < units:
                    ahead = scores_of(keys, unit + 1)
                else:
                    ahead = scores_of(keys_of(tile_of(jnp.minimum(turn + 1, count - 1))), 0)
                if masked:
                    visible = (key_pos >= begins[unit]) & (key_pos <= ends[unit])
                    scores = jnp.where(visible, scores, FLOOR_SCORE)
                before = peak[at]
                if fixed:
                    now, rescale = before, None
                else:
                    now = jnp.maximum(before, jnp.max(scores, axis=0, keepdims=True) * factor)
                    peak[at] = now
                    rescale = jnp.exp2(before - now)
                weights = jnp.exp2(scores * factor - now).astype(jnp.bfloat16)
                if waiting is not None:
                    gather(values, unit - 1, *waiting)
                else:
                    earlier = values_of(tile_of(jnp.maximum(turn - 1, 0)))
                    gather(earlier, units - 1, p_buf[:size], rescale_buf[...])
                waiting = weights, rescale
                scores = ahead
            s_buf[:size] = scores
            p_buf[:size] = waiting[0]
            if not fixed:
                rescale_buf[...] = waiting[1]
            return carried

        def whole():
            p_buf[:size] = jnp.zeros((size, cols), jnp.bfloat16)
            rescale_buf[...] = jnp.ones_like(rescale_buf)
            s_buf[:size] = scores_of(keys_of(tile_of(0)), 0)
            lax.fori_loop(0, count, step, 0)
            gather(values_of(tile_of(count - 1)), units - 1, p_buf[:size], rescale_buf[...])

        pl.when(count > 0)(whole)

    left = inner_lo - lo
    sweep(
        left + hi - inner_hi,
        lambda turn: jnp.where(turn < left, lo + turn, inner_hi + turn - left),
        edge_tile,
        True,
        False,
    )
    wait(late)
    sweep(
        (inner_hi - inner_lo) // ratio,
        lambda turn: inner_lo // ratio + turn,
        key_tile,
        False,
        True,
    )
    in_range = jnp.min(jnp.where(total[...] < SAFE_TOTAL, 1.0, 0.0))

    @pl.when(in_range < 0.5)
    def again():
        reset()
        sweep(hi - lo, lambda turn: lo + turn, edge_tile, True, False)

    for sub in range(subs):
        for group in range(groups):
            done = (acc[sub, group] * (1.0 / total[sub, group])).astype(jnp.bfloat16).T
            for member in range(PAIR):
                head = group * PAIR + member
                out_ref[sub * SUB : (sub + 1) * SUB, head * width : (head + 1) * width] = done[
                    member * SUB : (member + 1) * SUB
                ]


def attend(place, lengths, tasks, queries, kvs, subs, q_block):
    heads, _, width = queries.shape
    shard_rows = kvs[0].shape[1]
    slots = len(kvs)
    key_tile = min(KEY_TILE, shard_rows)
    edge_tile = min(EDGE_TILE, key_tile)
    groups, cols, rows = heads // PAIR, PAIR * SUB, subs * SUB
    return pl.pallas_call(
        partial(
            attend_kernel,
            slots=slots,
            subs=subs,
            q_block=q_block,
            key_tile=key_tile,
            edge_tile=edge_tile,
        ),
        grid_spec=pltpu.PrefetchScalarGridSpec(
            num_scalar_prefetch=3,
            grid=(1,),
            in_specs=[pl.BlockSpec(memory_space=pl.ANY)] * (1 + slots),
            out_specs=pl.BlockSpec((rows, heads * width), lambda i, *_: (0, 0)),
            scratch_shapes=[
                pltpu.VMEM((heads, rows, width), jnp.bfloat16),
                pltpu.VMEM((slots, 2, shard_rows, width), jnp.bfloat16),
                pltpu.VMEM((subs, groups, width, cols), jnp.float32),
                pltpu.VMEM((subs, groups, 1, cols), jnp.float32),
                pltpu.VMEM((subs, groups, 1, cols), jnp.float32),
                pltpu.VMEM((key_tile, cols), jnp.float32),
                pltpu.VMEM((key_tile, cols), jnp.bfloat16),
                pltpu.VMEM((1, cols), jnp.float32),
                pltpu.SemaphoreType.DMA((slots + 1,)),
            ],
        ),
        out_shape=jax.ShapeDtypeStruct((rows, heads * width), jnp.bfloat16),
        compiler_params=pltpu.CompilerParams(vmem_limit_bytes=VMEM_BYTES),
        cost_estimate=pl.CostEstimate(flops=rows, bytes_accessed=rows, transcendentals=0),
    )(place, lengths, tasks, queries, *kvs)


def local(queries, keys, values, doc_lengths, tasks, w_out):
    heads, tok_dev, width = queries.shape
    n_tok = lax.axis_size("tok")
    n_head = lax.axis_size("head")
    me = lax.axis_index("tok")
    z = lax.axis_index("head")
    tokens = n_tok * tok_dev
    q_block = tokens * heads // tasks.shape[0]
    chips = n_tok // 2
    doc_most = tokens * 4 // doc_lengths.shape[0]
    back = min(chips - 1, -(-(doc_most - 1) // (2 * tok_dev)))
    out_cols = w_out.shape[1] // n_head
    flat_tasks = tasks.reshape(-1)

    turned = values.reshape(-1, width, width).transpose(0, 2, 1).reshape(values.shape)
    own = jnp.concatenate([keys, turned], axis=0)
    spans = []
    for reach in range(back, 0, -1):
        pairs = [(i, i + 2 * reach) for i in range(n_tok - 2 * reach)]
        spans.append(lax.ppermute(own, "tok", pairs))

    def column(block):
        return lax.dynamic_slice_in_dim(w_out, block * out_cols, out_cols, 1)

    w_send = jnp.concatenate([column((z ^ 1) ^ 2), column(z ^ 1)], axis=1)
    w_pass, w_keep = column(z ^ 2), column(z)
    base = (me // 2 - back) * 2 * tok_dev
    starts = [tok_dev // SUB * sum(PARTS[:at]) // sum(PARTS) for at in range(len(PARTS) + 1)]
    places = []
    for at in starts[:-1]:
        numbers = [me % 2, me * tok_dev + at * SUB, base, at * SUB]
        places.append(jnp.stack([jnp.asarray(n, jnp.int32) for n in numbers]))
    spans, w_send, w_pass, w_keep, flat_tasks, places = lax.optimization_barrier(
        (spans, w_send, w_pass, w_keep, flat_tasks, places)
    )
    swap = [(i, i ^ 1) for i in range(n_tok)]
    kvs = []
    for mine in [*spans, own]:
        kvs += [mine, lax.ppermute(mine, "tok", swap)]

    near = [(i, i ^ 1) for i in range(n_head)]
    far = [(i, i ^ 2) for i in range(n_head)]

    def project(attended):
        sent = jnp.dot(attended, w_send, preferred_element_type=jnp.float32)
        return sent.astype(jnp.bfloat16)

    def onward(attended, arrived):
        summed = jnp.dot(attended, w_pass, preferred_element_type=jnp.float32)
        summed = summed + arrived[:, :out_cols].astype(jnp.float32)
        return summed.astype(jnp.bfloat16)

    def finish(attended, arrived, crossed):
        summed = jnp.dot(attended, w_keep, preferred_element_type=jnp.float32)
        summed = summed + arrived[:, out_cols:].astype(jnp.float32)
        return (summed + crossed.astype(jnp.float32)).astype(jnp.bfloat16)

    attended, sent, arrived, other, crossed = {}, {}, {}, {}, {}
    count = len(PARTS)
    for chunk in range(count):
        place = places[chunk]
        if chunk >= 1:
            place, sent[chunk - 1] = lax.optimization_barrier((place, sent[chunk - 1]))
            arrived[chunk - 1] = lax.ppermute(sent[chunk - 1], "head", near)
        if chunk >= LAG + 1:
            late = chunk - LAG - 1
            place, other[late] = lax.optimization_barrier((place, other[late]))
            crossed[late] = lax.ppermute(other[late], "head", far)
        subs = starts[chunk + 1] - starts[chunk]
        attended[chunk] = attend(
            place, doc_lengths, flat_tasks, queries, kvs, subs, q_block
        )
        sent[chunk] = project(attended[chunk])
        due = [chunk - LAG] if chunk < count - 1 else range(chunk - LAG, chunk)
        for late in due:
            if late >= 0:
                sent[chunk], arrived[late] = lax.optimization_barrier((sent[chunk], arrived[late]))
                other[late] = onward(attended[late], arrived[late])
        if chunk >= LAG + 1:
            late = chunk - LAG - 1
            sent[chunk], crossed[late] = lax.optimization_barrier((sent[chunk], crossed[late]))
    arrived[count - 1] = lax.ppermute(sent[count - 1], "head", near)
    for chunk in range(count):
        if chunk not in other:
            other[chunk] = onward(attended[chunk], arrived[chunk])
        if chunk not in crossed:
            crossed[chunk] = lax.ppermute(other[chunk], "head", far)
    outs = [finish(attended[c], arrived[c], crossed[c]) for c in range(count)]
    return jnp.concatenate(outs, axis=0)


def solution(mesh):
    placed = (
        P("head", "tok", None),
        P("head", "tok", None),
        P("head", "tok", None),
        P(),
        P(),
        P("head", None),
    )
    return jax.shard_map(
        local, mesh=mesh, in_specs=placed, out_specs=P("tok", "head"), check_vma=False
    )
```

```python
from functools import partial
import math

import jax
import jax.numpy as jnp
from jax import lax
from jax.experimental import pallas as pl
from jax.experimental.pallas import tpu as pltpu
from jax.sharding import PartitionSpec as P

FLOOR_SCORE = -1e30
SAFE_TOTAL = 2.0**100
KEY_TILE = 512
EDGE_TILE = 256
VMEM_BYTES = 40 * 2**20
SUB = 128
LAG = 1
PAIR = 4
PARTS = (1, 2, 2, 2, 1)


def attend_kernel(place, lengths, tasks, q_ref, *refs, slots, subs, q_block, key_tile, edge_tile):
    kv_refs, refs = refs[:slots], refs[slots:]
    out_ref, q_buf, kv_all, acc, peak, total, s_buf, p_buf, rescale_buf, sems = refs
    heads, _, width = q_ref.shape
    shard_rows = kv_refs[0].shape[1]
    groups = heads // PAIR
    units = subs * groups
    cols = PAIR * SUB
    rows = subs * SUB
    parity = place[0]
    first_row = place[1]
    base = place[2]
    q_copy = pltpu.make_async_copy(
        q_ref.at[:, pl.ds(pl.multiple_of(place[3], SUB), rows), :], q_buf, sems.at[slots]
    )
    q_copy.start()

    last_row = first_row + rows - 1
    one_head = [
        first_row + sub * SUB + lax.broadcasted_iota(jnp.int32, (1, SUB), 1) for sub in range(subs)
    ]
    begin = [jnp.zeros((1, SUB), jnp.int32)] * subs
    begin_first = jnp.int32(0)
    begin_last = jnp.int32(0)
    start = jnp.int32(0)
    for doc in range(lengths.shape[0]):
        begin = [
            jnp.where(one >= start, jnp.maximum(old, start), old)
            for one, old in zip(one_head, begin)
        ]
        begin_first = jnp.where(first_row >= start, jnp.maximum(begin_first, start), begin_first)
        begin_last = jnp.where(last_row >= start, jnp.maximum(begin_last, start), begin_last)
        start = start + lengths[doc]

    begins, ends, lows, highs = [], [], [], []
    for sub in range(subs):
        task = ((first_row + sub * SUB) // q_block) * heads
        low = [tasks[(task + head) * 5 + 2] * q_block for head in range(heads)]
        high = [tasks[(task + head) * 5 + 3] * q_block for head in range(heads)]
        for group in range(groups):
            members = range(group * PAIR, (group + 1) * PAIR)
            begins.append(
                jnp.concatenate([jnp.maximum(begin[sub], low[m]) for m in members], axis=1)
            )
            ends.append(
                jnp.concatenate([jnp.minimum(one_head[sub], high[m] - 1) for m in members], axis=1)
            )
        lows += low
        highs += high
    low_least, low_most, high_least, high_most = lows[0], lows[0], highs[0], highs[0]
    for low, high in zip(lows[1:], highs[1:]):
        low_least, low_most = jnp.minimum(low_least, low), jnp.maximum(low_most, low)
        high_least, high_most = jnp.minimum(high_least, high), jnp.maximum(high_most, high)

    ratio = key_tile // edge_tile
    tiles = slots * shard_rows // edge_tile
    lo = jnp.clip((jnp.maximum(low_least, begin_first) - base) // edge_tile, 0, tiles)
    hi = jnp.clip(
        (jnp.minimum(high_most, last_row + 1) - base + edge_tile - 1) // edge_tile, lo, tiles
    )
    full_lo = (jnp.maximum(low_most, begin_last) - base + key_tile - 1) // key_tile
    full_hi = (jnp.minimum(high_least, first_row + 1) - base) // key_tile
    full_lo = jnp.maximum(full_lo, 0)
    full_hi = jnp.minimum(full_hi, tiles // ratio)
    some = full_hi > full_lo
    inner_lo = jnp.where(some, full_lo * ratio, lo)
    inner_hi = jnp.where(some, full_hi * ratio, lo)
    factor = math.log2(math.e) / math.sqrt(width)

    def reset():
        acc[...] = jnp.zeros_like(acc)
        peak[...] = jnp.full_like(peak, FLOOR_SCORE)
        total[...] = jnp.zeros_like(total)

    per_slot = shard_rows // edge_tile
    early, late = [], []
    for at in range(slots):
        slot = at // 2 * 2 + (parity if at % 2 == 0 else 1 - parity)
        copy = pltpu.make_async_copy(kv_refs[at], kv_all.at[slot], sems.at[at])
        first, last = slot * per_slot, (slot + 1) * per_slot
        below = (lo < inner_lo) & (lo < last) & (inner_lo > first)
        above = (inner_hi < hi) & (inner_hi < last) & (hi > first)
        used = (lo < last) & (hi > first)
        early.append((below | above, copy))
        late.append((used & jnp.logical_not(below | above), copy))
    for needed, copy in early + late:
        pl.when(needed)(copy.start)

    def wait(copies):
        for needed, copy in copies:
            pl.when(needed)(copy.wait)

    reset()
    q_copy.wait()
    wait(early)

    def sweep(count, tile_of, size, masked, fixed):
        per_shard = shard_rows // size

        def keys_of(tile):
            offset = pl.multiple_of((tile % per_shard) * size, size)
            return kv_all[tile // per_shard, 0, pl.ds(offset, size), :]

        def values_of(tile):
            offset = pl.multiple_of((tile % per_shard) * size, size)
            values = kv_all[tile // per_shard, 1, pl.ds(offset, size), :]
            values = [values[at : at + width] for at in range(0, size, width)]
            values = jnp.concatenate(values, axis=1)
            return jnp.concatenate([values, jnp.ones((16, size), jnp.bfloat16)], axis=0)

        def scores_of(keys, unit):
            sub, group = divmod(unit, groups)
            asked = q_buf[group * PAIR : (group + 1) * PAIR, sub * SUB : (sub + 1) * SUB, :]
            return lax.dot_general(
                keys,
                asked.reshape(cols, width),
                (((1,), (1,)), ((), ())),
                preferred_element_type=jnp.float32,
            )

        def gather(values, unit, weights, rescale):
            at = divmod(unit, groups)
            product = lax.dot_general(
                values, weights, (((1,), (0,)), ((), ())), preferred_element_type=jnp.float32
            )
            if fixed:
                total[at] += product[width : width + 1]
                acc[at] += product[:width]
            else:
                total[at] = total[at] * rescale + product[width : width + 1]
                acc[at] = acc[at] * rescale + product[:width]

        def step(turn, carried):
            tile = tile_of(turn)
            keys, values = keys_of(tile), values_of(tile)
            key_pos = (
                base + tile * size + lax.broadcasted_iota(jnp.int32, (size, 1), 0)
                if masked
                else None
            )
            scores = s_buf[:size]
            waiting = None
            for unit in range(units):
                at = divmod(unit, groups)
                if unit + 1 < units:
                    ahead = scores_of(keys, unit + 1)
                else:
                    ahead = scores_of(keys_of(tile_of(jnp.minimum(turn + 1, count - 1))), 0)
                if masked:
                    visible = (key_pos >= begins[unit]) & (key_pos <= ends[unit])
                    scores = jnp.where(visible, scores, FLOOR_SCORE)
                before = peak[at]
                if fixed:
                    now, rescale = before, None
                else:
                    now = jnp.maximum(before, jnp.max(scores, axis=0, keepdims=True) * factor)
                    peak[at] = now
                    rescale = jnp.exp2(before - now)
                weights = jnp.exp2(scores * factor - now).astype(jnp.bfloat16)
                if waiting is not None:
                    gather(values, unit - 1, *waiting)
                else:
                    earlier = values_of(tile_of(jnp.maximum(turn - 1, 0)))
                    gather(earlier, units - 1, p_buf[:size], rescale_buf[...])
                waiting = weights, rescale
                scores = ahead
            s_buf[:size] = scores
            p_buf[:size] = waiting[0]
            if not fixed:
                rescale_buf[...] = waiting[1]
            return carried

        def whole():
            p_buf[:size] = jnp.zeros((size, cols), jnp.bfloat16)
            rescale_buf[...] = jnp.ones_like(rescale_buf)
            s_buf[:size] = scores_of(keys_of(tile_of(0)), 0)
            lax.fori_loop(0, count, step, 0)
            gather(values_of(tile_of(count - 1)), units - 1, p_buf[:size], rescale_buf[...])

        pl.when(count > 0)(whole)

    left = inner_lo - lo
    sweep(
        left + hi - inner_hi,
        lambda turn: jnp.where(turn < left, lo + turn, inner_hi + turn - left),
        edge_tile,
        True,
        False,
    )
    wait(late)
    sweep(
        (inner_hi - inner_lo) // ratio,
        lambda turn: inner_lo // ratio + turn,
        key_tile,
        False,
        True,
    )
    in_range = jnp.min(jnp.where(total[...] < SAFE_TOTAL, 1.0, 0.0))

    @pl.when(in_range < 0.5)
    def again():
        reset()
        sweep(hi - lo, lambda turn: lo + turn, edge_tile, True, False)

    for sub in range(subs):
        for group in range(groups):
            done = (acc[sub, group] * (1.0 / total[sub, group])).astype(jnp.bfloat16).T
            for member in range(PAIR):
                head = group * PAIR + member
                out_ref[sub * SUB : (sub + 1) * SUB, head * width : (head + 1) * width] = done[
                    member * SUB : (member + 1) * SUB
                ]


def attend(place, lengths, tasks, queries, kvs, subs, q_block):
    heads, _, width = queries.shape
    shard_rows = kvs[0].shape[1]
    slots = len(kvs)
    key_tile = min(KEY_TILE, shard_rows)
    edge_tile = min(EDGE_TILE, key_tile)
    groups, cols, rows = heads // PAIR, PAIR * SUB, subs * SUB
    return pl.pallas_call(
        partial(
            attend_kernel,
            slots=slots,
            subs=subs,
            q_block=q_block,
            key_tile=key_tile,
            edge_tile=edge_tile,
        ),
        grid_spec=pltpu.PrefetchScalarGridSpec(
            num_scalar_prefetch=3,
            grid=(1,),
            in_specs=[pl.BlockSpec(memory_space=pl.ANY)] * (1 + slots),
            out_specs=pl.BlockSpec((rows, heads * width), lambda i, *_: (0, 0)),
            scratch_shapes=[
                pltpu.VMEM((heads, rows, width), jnp.bfloat16),
                pltpu.VMEM((slots, 2, shard_rows, width), jnp.bfloat16),
                pltpu.VMEM((subs, groups, width, cols), jnp.float32),
                pltpu.VMEM((subs, groups, 1, cols), jnp.float32),
                pltpu.VMEM((subs, groups, 1, cols), jnp.float32),
                pltpu.VMEM((key_tile, cols), jnp.float32),
                pltpu.VMEM((key_tile, cols), jnp.bfloat16),
                pltpu.VMEM((1, cols), jnp.float32),
                pltpu.SemaphoreType.DMA((slots + 1,)),
            ],
        ),
        out_shape=jax.ShapeDtypeStruct((rows, heads * width), jnp.bfloat16),
        compiler_params=pltpu.CompilerParams(vmem_limit_bytes=VMEM_BYTES),
        cost_estimate=pl.CostEstimate(flops=rows, bytes_accessed=rows, transcendentals=0),
    )(place, lengths, tasks, queries, *kvs)


def local(queries, keys, values, doc_lengths, tasks, w_out):
    heads, tok_dev, width = queries.shape
    n_tok = lax.axis_size("tok")
    n_head = lax.axis_size("head")
    me = lax.axis_index("tok")
    z = lax.axis_index("head")
    tokens = n_tok * tok_dev
    q_block = tokens * heads // tasks.shape[0]
    chips = n_tok // 2
    doc_most = tokens * 4 // doc_lengths.shape[0]
    back = min(chips - 1, -(-(doc_most - 1) // (2 * tok_dev)))
    out_cols = w_out.shape[1] // n_head
    flat_tasks = tasks.reshape(-1)

    turned = values.reshape(-1, width, width).transpose(0, 2, 1).reshape(values.shape)
    own = jnp.concatenate([keys, turned], axis=0)
    spans = []
    for reach in range(back, 0, -1):
        pairs = [(i, i + 2 * reach) for i in range(n_tok - 2 * reach)]
        spans.append(lax.ppermute(own, "tok", pairs))

    def column(block):
        return lax.dynamic_slice_in_dim(w_out, block * out_cols, out_cols, 1)

    w_send = jnp.concatenate([column((z ^ 1) ^ 2), column(z ^ 1)], axis=1)
    w_pass, w_keep = column(z ^ 2), column(z)
    base = (me // 2 - back) * 2 * tok_dev
    starts = [tok_dev // SUB * sum(PARTS[:at]) // sum(PARTS) for at in range(len(PARTS) + 1)]
    places = []
    for at in starts[:-1]:
        numbers = [me % 2, me * tok_dev + at * SUB, base, at * SUB]
        places.append(jnp.stack([jnp.asarray(n, jnp.int32) for n in numbers]))
    spans, w_send, w_pass, w_keep, flat_tasks, places = lax.optimization_barrier(
        (spans, w_send, w_pass, w_keep, flat_tasks, places)
    )
    swap = [(i, i ^ 1) for i in range(n_tok)]
    kvs = []
    for mine in [*spans, own]:
        kvs += [mine, lax.ppermute(mine, "tok", swap)]

    near = [(i, i ^ 1) for i in range(n_head)]
    far = [(i, i ^ 2) for i in range(n_head)]

    def project(attended):
        sent = jnp.dot(attended, w_send, preferred_element_type=jnp.float32)
        return sent.astype(jnp.bfloat16)

    def onward(attended, arrived):
        summed = jnp.dot(attended, w_pass, preferred_element_type=jnp.float32)
        summed = summed + arrived[:, :out_cols].astype(jnp.float32)
        return summed.astype(jnp.bfloat16)

    def finish(attended, arrived, crossed):
        summed = jnp.dot(attended, w_keep, preferred_element_type=jnp.float32)
        summed = summed + arrived[:, out_cols:].astype(jnp.float32)
        return (summed + crossed.astype(jnp.float32)).astype(jnp.bfloat16)

    attended, sent, arrived, other, crossed = {}, {}, {}, {}, {}
    count = len(PARTS)
    for chunk in range(count):
        place = places[chunk]
        if chunk >= 1:
            place, sent[chunk - 1] = lax.optimization_barrier((place, sent[chunk - 1]))
            arrived[chunk - 1] = lax.ppermute(sent[chunk - 1], "head", near)
        if chunk >= LAG + 1:
            late = chunk - LAG - 1
            place, other[late] = lax.optimization_barrier((place, other[late]))
            crossed[late] = lax.ppermute(other[late], "head", far)
        subs = starts[chunk + 1] - starts[chunk]
        attended[chunk] = attend(
            place, doc_lengths, flat_tasks, queries, kvs, subs, q_block
        )
        sent[chunk] = project(attended[chunk])
        if chunk >= LAG:
            late = chunk - LAG
            sent[chunk], arrived[late] = lax.optimization_barrier((sent[chunk], arrived[late]))
            other[late] = onward(attended[late], arrived[late])
            if late - 1 in crossed:
                sent[chunk], crossed[late - 1] = lax.optimization_barrier(
                    (sent[chunk], crossed[late - 1])
                )
    arrived[count - 1] = lax.ppermute(sent[count - 1], "head", near)
    for chunk in range(count):
        if chunk not in other:
            other[chunk] = onward(attended[chunk], arrived[chunk])
        if chunk not in crossed:
            crossed[chunk] = lax.ppermute(other[chunk], "head", far)
    outs = [finish(attended[c], arrived[c], crossed[c]) for c in range(count)]
    return jnp.concatenate(outs, axis=0)


def solution(mesh):
    placed = (
        P("head", "tok", None),
        P("head", "tok", None),
        P("head", "tok", None),
        P(),
        P(),
        P("head", None),
    )
    return jax.shard_map(
        local, mesh=mesh, in_specs=placed, out_specs=P("tok", "head"), check_vma=False
    )
```

```python
from functools import partial
import math

import jax
import jax.numpy as jnp
from jax import lax
from jax.experimental import pallas as pl
from jax.experimental.pallas import tpu as pltpu
from jax.sharding import PartitionSpec as P

FLOOR_SCORE = -1e30
SAFE_TOTAL = 2.0**100
KEY_TILE = 512
EDGE_TILE = 256
VMEM_BYTES = 40 * 2**20
SUB = 128
LAG = 1
PAIR = 4
PARTS = (1, 2, 2, 2, 1)


def attend_kernel(place, lengths, tasks, q_ref, *refs, slots, subs, q_block, key_tile, edge_tile):
    kv_refs, refs = refs[:slots], refs[slots:]
    out_ref, q_buf, kv_all, acc, peak, total, s_buf, p_buf, rescale_buf, sems = refs
    heads, _, width = q_ref.shape
    shard_rows = kv_refs[0].shape[1]
    groups = heads // PAIR
    units = subs * groups
    cols = PAIR * SUB
    rows = subs * SUB
    parity = place[0]
    first_row = place[1]
    base = place[2]
    q_copy = pltpu.make_async_copy(
        q_ref.at[:, pl.ds(pl.multiple_of(place[3], SUB), rows), :], q_buf, sems.at[slots]
    )
    q_copy.start()

    last_row = first_row + rows - 1
    one_head = [
        first_row + sub * SUB + lax.broadcasted_iota(jnp.int32, (1, SUB), 1) for sub in range(subs)
    ]
    begin = [jnp.zeros((1, SUB), jnp.int32)] * subs
    begin_first = jnp.int32(0)
    begin_last = jnp.int32(0)
    start = jnp.int32(0)
    for doc in range(lengths.shape[0]):
        begin = [
            jnp.where(one >= start, jnp.maximum(old, start), old)
            for one, old in zip(one_head, begin)
        ]
        begin_first = jnp.where(first_row >= start, jnp.maximum(begin_first, start), begin_first)
        begin_last = jnp.where(last_row >= start, jnp.maximum(begin_last, start), begin_last)
        start = start + lengths[doc]

    begins, ends, lows, highs = [], [], [], []
    for sub in range(subs):
        task = ((first_row + sub * SUB) // q_block) * heads
        low = [tasks[(task + head) * 5 + 2] * q_block for head in range(heads)]
        high = [tasks[(task + head) * 5 + 3] * q_block for head in range(heads)]
        for group in range(groups):
            members = range(group * PAIR, (group + 1) * PAIR)
            begins.append(
                jnp.concatenate([jnp.maximum(begin[sub], low[m]) for m in members], axis=1)
            )
            ends.append(
                jnp.concatenate([jnp.minimum(one_head[sub], high[m] - 1) for m in members], axis=1)
            )
        lows += low
        highs += high
    low_least, low_most, high_least, high_most = lows[0], lows[0], highs[0], highs[0]
    for low, high in zip(lows[1:], highs[1:]):
        low_least, low_most = jnp.minimum(low_least, low), jnp.maximum(low_most, low)
        high_least, high_most = jnp.minimum(high_least, high), jnp.maximum(high_most, high)

    ratio = key_tile // edge_tile
    tiles = slots * shard_rows // edge_tile
    lo = jnp.clip((jnp.maximum(low_least, begin_first) - base) // edge_tile, 0, tiles)
    hi = jnp.clip(
        (jnp.minimum(high_most, last_row + 1) - base + edge_tile - 1) // edge_tile, lo, tiles
    )
    far_lo = lo // ratio
    far_hi = jnp.maximum((jnp.minimum(high_least, first_row) - base) // key_tile, far_lo)
    clear_lo = (jnp.maximum(low_most, begin_last) - base + key_tile - 1) // key_tile
    clear_lo = jnp.clip(clear_lo, far_lo, far_hi)
    near_lo = jnp.maximum(lo, far_hi * ratio)
    factor = math.log2(math.e) / math.sqrt(width)

    def reset():
        acc[...] = jnp.zeros_like(acc)
        peak[...] = jnp.full_like(peak, FLOOR_SCORE)
        total[...] = jnp.zeros_like(total)

    per_slot = shard_rows // edge_tile
    early, late = [], []
    for at in range(slots):
        slot = at // 2 * 2 + (parity if at % 2 == 0 else 1 - parity)
        copy = pltpu.make_async_copy(kv_refs[at], kv_all.at[slot], sems.at[at])
        first, last = slot * per_slot, (slot + 1) * per_slot
        soon = (near_lo < last) & (hi > first)
        used = (far_lo * ratio < last) & (hi > first)
        early.append((soon, copy))
        late.append((used & jnp.logical_not(soon), copy))
    for needed, copy in early + late:
        pl.when(needed)(copy.start)

    def wait(copies):
        for needed, copy in copies:
            pl.when(needed)(copy.wait)

    reset()
    q_copy.wait()
    wait(early)

    def sweep(count, tile_of, size, masked, fixed):
        per_shard = shard_rows // size

        def keys_of(tile):
            offset = pl.multiple_of((tile % per_shard) * size, size)
            return kv_all[tile // per_shard, 0, pl.ds(offset, size), :]

        def values_of(tile):
            offset = pl.multiple_of((tile % per_shard) * size, size)
            values = kv_all[tile // per_shard, 1, pl.ds(offset, size), :]
            values = [values[at : at + width] for at in range(0, size, width)]
            values = jnp.concatenate(values, axis=1)
            return jnp.concatenate([values, jnp.ones((16, size), jnp.bfloat16)], axis=0)

        def scores_of(keys, unit):
            sub, group = divmod(unit, groups)
            asked = q_buf[group * PAIR : (group + 1) * PAIR, sub * SUB : (sub + 1) * SUB, :]
            return lax.dot_general(
                keys,
                asked.reshape(cols, width),
                (((1,), (1,)), ((), ())),
                preferred_element_type=jnp.float32,
            )

        def gather(values, unit, weights, rescale):
            at = divmod(unit, groups)
            product = lax.dot_general(
                values, weights, (((1,), (0,)), ((), ())), preferred_element_type=jnp.float32
            )
            if fixed:
                total[at] += product[width : width + 1]
                acc[at] += product[:width]
            else:
                total[at] = total[at] * rescale + product[width : width + 1]
                acc[at] = acc[at] * rescale + product[:width]

        def step(turn, carried):
            tile = tile_of(turn)
            keys, values = keys_of(tile), values_of(tile)
            key_pos = (
                base + tile * size + lax.broadcasted_iota(jnp.int32, (size, 1), 0)
                if masked
                else None
            )
            scores = s_buf[:size]
            waiting = None
            for unit in range(units):
                at = divmod(unit, groups)
                if unit + 1 < units:
                    ahead = scores_of(keys, unit + 1)
                else:
                    ahead = scores_of(keys_of(tile_of(jnp.minimum(turn + 1, count - 1))), 0)
                if masked:
                    visible = (key_pos >= begins[unit]) & (key_pos <= ends[unit])
                    scores = jnp.where(visible, scores, FLOOR_SCORE)
                before = peak[at]
                if fixed:
                    now, rescale = before, None
                else:
                    now = jnp.maximum(before, jnp.max(scores, axis=0, keepdims=True) * factor)
                    peak[at] = now
                    rescale = jnp.exp2(before - now)
                weights = jnp.exp2(scores * factor - now).astype(jnp.bfloat16)
                if waiting is not None:
                    gather(values, unit - 1, *waiting)
                else:
                    earlier = values_of(tile_of(jnp.maximum(turn - 1, 0)))
                    gather(earlier, units - 1, p_buf[:size], rescale_buf[...])
                waiting = weights, rescale
                scores = ahead
            s_buf[:size] = scores
            p_buf[:size] = waiting[0]
            if not fixed:
                rescale_buf[...] = waiting[1]
            return carried

        def whole():
            p_buf[:size] = jnp.zeros((size, cols), jnp.bfloat16)
            rescale_buf[...] = jnp.ones_like(rescale_buf)
            s_buf[:size] = scores_of(keys_of(tile_of(0)), 0)
            lax.fori_loop(0, count, step, 0)
            gather(values_of(tile_of(count - 1)), units - 1, p_buf[:size], rescale_buf[...])

        pl.when(count > 0)(whole)

    sweep(hi - near_lo, lambda turn: near_lo + turn, edge_tile, True, False)
    wait(late)
    sweep(far_hi - clear_lo, lambda turn: clear_lo + turn, key_tile, False, True)
    sweep(clear_lo - far_lo, lambda turn: far_lo + turn, key_tile, True, True)
    in_range = jnp.min(jnp.where(total[...] < SAFE_TOTAL, 1.0, 0.0))

    @pl.when(in_range < 0.5)
    def again():
        reset()
        sweep(hi - lo, lambda turn: lo + turn, edge_tile, True, False)

    for sub in range(subs):
        for group in range(groups):
            done = (acc[sub, group] * (1.0 / total[sub, group])).astype(jnp.bfloat16).T
            for member in range(PAIR):
                head = group * PAIR + member
                out_ref[sub * SUB : (sub + 1) * SUB, head * width : (head + 1) * width] = done[
                    member * SUB : (member + 1) * SUB
                ]


def attend(place, lengths, tasks, queries, kvs, subs, q_block):
    heads, _, width = queries.shape
    shard_rows = kvs[0].shape[1]
    slots = len(kvs)
    key_tile = min(KEY_TILE, shard_rows)
    edge_tile = min(EDGE_TILE, key_tile)
    groups, cols, rows = heads // PAIR, PAIR * SUB, subs * SUB
    return pl.pallas_call(
        partial(
            attend_kernel,
            slots=slots,
            subs=subs,
            q_block=q_block,
            key_tile=key_tile,
            edge_tile=edge_tile,
        ),
        grid_spec=pltpu.PrefetchScalarGridSpec(
            num_scalar_prefetch=3,
            grid=(1,),
            in_specs=[pl.BlockSpec(memory_space=pl.ANY)] * (1 + slots),
            out_specs=pl.BlockSpec((rows, heads * width), lambda i, *_: (0, 0)),
            scratch_shapes=[
                pltpu.VMEM((heads, rows, width), jnp.bfloat16),
                pltpu.VMEM((slots, 2, shard_rows, width), jnp.bfloat16),
                pltpu.VMEM((subs, groups, width, cols), jnp.float32),
                pltpu.VMEM((subs, groups, 1, cols), jnp.float32),
                pltpu.VMEM((subs, groups, 1, cols), jnp.float32),
                pltpu.VMEM((key_tile, cols), jnp.float32),
                pltpu.VMEM((key_tile, cols), jnp.bfloat16),
                pltpu.VMEM((1, cols), jnp.float32),
                pltpu.SemaphoreType.DMA((slots + 1,)),
            ],
        ),
        out_shape=jax.ShapeDtypeStruct((rows, heads * width), jnp.bfloat16),
        compiler_params=pltpu.CompilerParams(vmem_limit_bytes=VMEM_BYTES),
        cost_estimate=pl.CostEstimate(flops=rows, bytes_accessed=rows, transcendentals=0),
    )(place, lengths, tasks, queries, *kvs)


def local(queries, keys, values, doc_lengths, tasks, w_out):
    heads, tok_dev, width = queries.shape
    n_tok = lax.axis_size("tok")
    n_head = lax.axis_size("head")
    me = lax.axis_index("tok")
    z = lax.axis_index("head")
    tokens = n_tok * tok_dev
    q_block = tokens * heads // tasks.shape[0]
    chips = n_tok // 2
    doc_most = tokens * 4 // doc_lengths.shape[0]
    back = min(chips - 1, -(-(doc_most - 1) // (2 * tok_dev)))
    out_cols = w_out.shape[1] // n_head
    flat_tasks = tasks.reshape(-1)

    turned = values.reshape(-1, width, width).transpose(0, 2, 1).reshape(values.shape)
    own = jnp.concatenate([keys, turned], axis=0)
    spans = []
    for reach in range(back, 0, -1):
        pairs = [(i, i + 2 * reach) for i in range(n_tok - 2 * reach)]
        spans.append(lax.ppermute(own, "tok", pairs))

    def column(block):
        return lax.dynamic_slice_in_dim(w_out, block * out_cols, out_cols, 1)

    w_send = jnp.concatenate([column((z ^ 1) ^ 2), column(z ^ 1)], axis=1)
    w_pass, w_keep = column(z ^ 2), column(z)
    base = (me // 2 - back) * 2 * tok_dev
    starts = [tok_dev // SUB * sum(PARTS[:at]) // sum(PARTS) for at in range(len(PARTS) + 1)]
    places = []
    for at in starts[:-1]:
        numbers = [me % 2, me * tok_dev + at * SUB, base, at * SUB]
        places.append(jnp.stack([jnp.asarray(n, jnp.int32) for n in numbers]))
    spans, w_send, w_pass, w_keep, flat_tasks, places = lax.optimization_barrier(
        (spans, w_send, w_pass, w_keep, flat_tasks, places)
    )
    swap = [(i, i ^ 1) for i in range(n_tok)]
    kvs = []
    for mine in [*spans, own]:
        kvs += [mine, lax.ppermute(mine, "tok", swap)]

    near = [(i, i ^ 1) for i in range(n_head)]
    far = [(i, i ^ 2) for i in range(n_head)]

    def project(attended):
        sent = jnp.dot(attended, w_send, preferred_element_type=jnp.float32)
        return sent.astype(jnp.bfloat16)

    def onward(attended, arrived):
        summed = jnp.dot(attended, w_pass, preferred_element_type=jnp.float32)
        summed = summed + arrived[:, :out_cols].astype(jnp.float32)
        return summed.astype(jnp.bfloat16)

    def finish(attended, arrived, crossed):
        summed = jnp.dot(attended, w_keep, preferred_element_type=jnp.float32)
        summed = summed + arrived[:, out_cols:].astype(jnp.float32)
        return (summed + crossed.astype(jnp.float32)).astype(jnp.bfloat16)

    attended, sent, arrived, other, crossed = {}, {}, {}, {}, {}
    count = len(PARTS)
    for chunk in range(count):
        place = places[chunk]
        if chunk >= 1:
            place, sent[chunk - 1] = lax.optimization_barrier((place, sent[chunk - 1]))
            arrived[chunk - 1] = lax.ppermute(sent[chunk - 1], "head", near)
        if chunk >= LAG + 1:
            late = chunk - LAG - 1
            place, other[late] = lax.optimization_barrier((place, other[late]))
            crossed[late] = lax.ppermute(other[late], "head", far)
        subs = starts[chunk + 1] - starts[chunk]
        attended[chunk] = attend(
            place, doc_lengths, flat_tasks, queries, kvs, subs, q_block
        )
        sent[chunk] = project(attended[chunk])
        if chunk >= LAG:
            late = chunk - LAG
            sent[chunk], arrived[late] = lax.optimization_barrier((sent[chunk], arrived[late]))
            other[late] = onward(attended[late], arrived[late])
            if late - 1 in crossed:
                sent[chunk], crossed[late - 1] = lax.optimization_barrier(
                    (sent[chunk], crossed[late - 1])
                )
    arrived[count - 1] = lax.ppermute(sent[count - 1], "head", near)
    for chunk in range(count):
        if chunk not in other:
            other[chunk] = onward(attended[chunk], arrived[chunk])
        if chunk not in crossed:
            crossed[chunk] = lax.ppermute(other[chunk], "head", far)
    outs = [finish(attended[c], arrived[c], crossed[c]) for c in range(count)]
    return jnp.concatenate(outs, axis=0)


def solution(mesh):
    placed = (
        P("head", "tok", None),
        P("head", "tok", None),
        P("head", "tok", None),
        P(),
        P(),
        P("head", None),
    )
    return jax.shard_map(
        local, mesh=mesh, in_specs=placed, out_specs=P("tok", "head"), check_vma=False
    )
```

```python
from functools import partial
import math

import jax
import jax.numpy as jnp
from jax import lax
from jax.experimental import pallas as pl
from jax.experimental.pallas import tpu as pltpu
from jax.sharding import PartitionSpec as P

FLOOR_SCORE = -1e30
SAFE_TOTAL = 2.0**100
KEY_TILE = 512
EDGE_TILE = 256
VMEM_BYTES = 40 * 2**20
SUB = 128
LAG = 1
PAIR = 4
PARTS = (2, 2, 2, 2)


def attend_kernel(place, lengths, tasks, q_ref, *refs, slots, subs, q_block, key_tile, edge_tile):
    kv_refs, refs = refs[:slots], refs[slots:]
    out_ref, q_buf, kv_all, acc, peak, total, s_buf, p_buf, rescale_buf, sems = refs
    heads, _, width = q_ref.shape
    shard_rows = kv_refs[0].shape[1]
    groups = heads // PAIR
    units = subs * groups
    cols = PAIR * SUB
    rows = subs * SUB
    parity = place[0]
    first_row = place[1]
    base = place[2]
    q_copy = pltpu.make_async_copy(
        q_ref.at[:, pl.ds(pl.multiple_of(place[3], SUB), rows), :], q_buf, sems.at[slots]
    )
    q_copy.start()

    last_row = first_row + rows - 1
    one_head = [
        first_row + sub * SUB + lax.broadcasted_iota(jnp.int32, (1, SUB), 1) for sub in range(subs)
    ]
    begin = [jnp.zeros((1, SUB), jnp.int32)] * subs
    begin_first = jnp.int32(0)
    begin_last = jnp.int32(0)
    start = jnp.int32(0)
    for doc in range(lengths.shape[0]):
        begin = [
            jnp.where(one >= start, jnp.maximum(old, start), old)
            for one, old in zip(one_head, begin)
        ]
        begin_first = jnp.where(first_row >= start, jnp.maximum(begin_first, start), begin_first)
        begin_last = jnp.where(last_row >= start, jnp.maximum(begin_last, start), begin_last)
        start = start + lengths[doc]

    begins, ends, lows, highs = [], [], [], []
    for sub in range(subs):
        task = ((first_row + sub * SUB) // q_block) * heads
        low = [tasks[(task + head) * 5 + 2] * q_block for head in range(heads)]
        high = [tasks[(task + head) * 5 + 3] * q_block for head in range(heads)]
        for group in range(groups):
            members = range(group * PAIR, (group + 1) * PAIR)
            begins.append(
                jnp.concatenate([jnp.maximum(begin[sub], low[m]) for m in members], axis=1)
            )
            ends.append(
                jnp.concatenate([jnp.minimum(one_head[sub], high[m] - 1) for m in members], axis=1)
            )
        lows += low
        highs += high
    low_least, low_most, high_least, high_most = lows[0], lows[0], highs[0], highs[0]
    for low, high in zip(lows[1:], highs[1:]):
        low_least, low_most = jnp.minimum(low_least, low), jnp.maximum(low_most, low)
        high_least, high_most = jnp.minimum(high_least, high), jnp.maximum(high_most, high)

    ratio = key_tile // edge_tile
    tiles = slots * shard_rows // edge_tile
    lo = jnp.clip((jnp.maximum(low_least, begin_first) - base) // edge_tile, 0, tiles)
    hi = jnp.clip(
        (jnp.minimum(high_most, last_row + 1) - base + edge_tile - 1) // edge_tile, lo, tiles
    )
    far_lo = lo // ratio
    far_hi = jnp.maximum((jnp.minimum(high_least, first_row) - base) // key_tile, far_lo)
    clear_lo = (jnp.maximum(low_most, begin_last) - base + key_tile - 1) // key_tile
    clear_lo = jnp.clip(clear_lo, far_lo, far_hi)
    near_lo = jnp.maximum(lo, far_hi * ratio)
    factor = math.log2(math.e) / math.sqrt(width)

    def reset():
        acc[...] = jnp.zeros_like(acc)
        peak[...] = jnp.full_like(peak, FLOOR_SCORE)
        total[...] = jnp.zeros_like(total)

    per_slot = shard_rows // edge_tile
    early, late = [], []
    for at in range(slots):
        slot = at // 2 * 2 + (parity if at % 2 == 0 else 1 - parity)
        copy = pltpu.make_async_copy(kv_refs[at], kv_all.at[slot], sems.at[at])
        first, last = slot * per_slot, (slot + 1) * per_slot
        soon = (near_lo < last) & (hi > first)
        used = (far_lo * ratio < last) & (hi > first)
        early.append((soon, copy))
        late.append((used & jnp.logical_not(soon), copy))
    for needed, copy in early + late:
        pl.when(needed)(copy.start)

    def wait(copies):
        for needed, copy in copies:
            pl.when(needed)(copy.wait)

    reset()
    q_copy.wait()
    wait(early)

    def sweep(count, tile_of, size, masked, fixed):
        per_shard = shard_rows // size

        def keys_of(tile):
            offset = pl.multiple_of((tile % per_shard) * size, size)
            return kv_all[tile // per_shard, 0, pl.ds(offset, size), :]

        def values_of(tile):
            offset = pl.multiple_of((tile % per_shard) * size, size)
            values = kv_all[tile // per_shard, 1, pl.ds(offset, size), :]
            values = [values[at : at + width] for at in range(0, size, width)]
            values = jnp.concatenate(values, axis=1)
            return jnp.concatenate([values, jnp.ones((16, size), jnp.bfloat16)], axis=0)

        def scores_of(keys, unit):
            sub, group = divmod(unit, groups)
            asked = q_buf[group * PAIR : (group + 1) * PAIR, sub * SUB : (sub + 1) * SUB, :]
            return lax.dot_general(
                keys,
                asked.reshape(cols, width),
                (((1,), (1,)), ((), ())),
                preferred_element_type=jnp.float32,
            )

        def gather(values, unit, weights, rescale):
            at = divmod(unit, groups)
            product = lax.dot_general(
                values, weights, (((1,), (0,)), ((), ())), preferred_element_type=jnp.float32
            )
            if fixed:
                total[at] += product[width : width + 1]
                acc[at] += product[:width]
            else:
                total[at] = total[at] * rescale + product[width : width + 1]
                acc[at] = acc[at] * rescale + product[:width]

        def step(turn, carried):
            tile = tile_of(turn)
            keys, values = keys_of(tile), values_of(tile)
            key_pos = (
                base + tile * size + lax.broadcasted_iota(jnp.int32, (size, 1), 0)
                if masked
                else None
            )
            scores = s_buf[:size]
            waiting = None
            for unit in range(units):
                at = divmod(unit, groups)
                if unit + 1 < units:
                    ahead = scores_of(keys, unit + 1)
                else:
                    ahead = scores_of(keys_of(tile_of(jnp.minimum(turn + 1, count - 1))), 0)
                if masked:
                    visible = (key_pos >= begins[unit]) & (key_pos <= ends[unit])
                    scores = jnp.where(visible, scores, FLOOR_SCORE)
                before = peak[at]
                if fixed:
                    now, rescale = before, None
                else:
                    now = jnp.maximum(before, jnp.max(scores, axis=0, keepdims=True) * factor)
                    peak[at] = now
                    rescale = jnp.exp2(before - now)
                weights = jnp.exp2(scores * factor - now).astype(jnp.bfloat16)
                if waiting is not None:
                    gather(values, unit - 1, *waiting)
                else:
                    earlier = values_of(tile_of(jnp.maximum(turn - 1, 0)))
                    gather(earlier, units - 1, p_buf[:size], rescale_buf[...])
                waiting = weights, rescale
                scores = ahead
            s_buf[:size] = scores
            p_buf[:size] = waiting[0]
            if not fixed:
                rescale_buf[...] = waiting[1]
            return carried

        def whole():
            p_buf[:size] = jnp.zeros((size, cols), jnp.bfloat16)
            rescale_buf[...] = jnp.ones_like(rescale_buf)
            s_buf[:size] = scores_of(keys_of(tile_of(0)), 0)
            lax.fori_loop(0, count, step, 0)
            gather(values_of(tile_of(count - 1)), units - 1, p_buf[:size], rescale_buf[...])

        pl.when(count > 0)(whole)

    sweep(hi - near_lo, lambda turn: near_lo + turn, edge_tile, True, False)
    wait(late)
    sweep(far_hi - clear_lo, lambda turn: clear_lo + turn, key_tile, False, True)
    sweep(clear_lo - far_lo, lambda turn: far_lo + turn, key_tile, True, True)
    in_range = jnp.min(jnp.where(total[...] < SAFE_TOTAL, 1.0, 0.0))

    @pl.when(in_range < 0.5)
    def again():
        reset()
        sweep(hi - lo, lambda turn: lo + turn, edge_tile, True, False)

    for sub in range(subs):
        for group in range(groups):
            done = (acc[sub, group] * (1.0 / total[sub, group])).astype(jnp.bfloat16).T
            for member in range(PAIR):
                head = group * PAIR + member
                out_ref[sub * SUB : (sub + 1) * SUB, head * width : (head + 1) * width] = done[
                    member * SUB : (member + 1) * SUB
                ]


def attend(place, lengths, tasks, queries, kvs, subs, q_block):
    heads, _, width = queries.shape
    shard_rows = kvs[0].shape[1]
    slots = len(kvs)
    key_tile = min(KEY_TILE, shard_rows)
    edge_tile = min(EDGE_TILE, key_tile)
    groups, cols, rows = heads // PAIR, PAIR * SUB, subs * SUB
    return pl.pallas_call(
        partial(
            attend_kernel,
            slots=slots,
            subs=subs,
            q_block=q_block,
            key_tile=key_tile,
            edge_tile=edge_tile,
        ),
        grid_spec=pltpu.PrefetchScalarGridSpec(
            num_scalar_prefetch=3,
            grid=(1,),
            in_specs=[pl.BlockSpec(memory_space=pl.ANY)] * (1 + slots),
            out_specs=pl.BlockSpec((rows, heads * width), lambda i, *_: (0, 0)),
            scratch_shapes=[
                pltpu.VMEM((heads, rows, width), jnp.bfloat16),
                pltpu.VMEM((slots, 2, shard_rows, width), jnp.bfloat16),
                pltpu.VMEM((subs, groups, width, cols), jnp.float32),
                pltpu.VMEM((subs, groups, 1, cols), jnp.float32),
                pltpu.VMEM((subs, groups, 1, cols), jnp.float32),
                pltpu.VMEM((key_tile, cols), jnp.float32),
                pltpu.VMEM((key_tile, cols), jnp.bfloat16),
                pltpu.VMEM((1, cols), jnp.float32),
                pltpu.SemaphoreType.DMA((slots + 1,)),
            ],
        ),
        out_shape=jax.ShapeDtypeStruct((rows, heads * width), jnp.bfloat16),
        compiler_params=pltpu.CompilerParams(vmem_limit_bytes=VMEM_BYTES),
        cost_estimate=pl.CostEstimate(flops=rows, bytes_accessed=rows, transcendentals=0),
    )(place, lengths, tasks, queries, *kvs)


def local(queries, keys, values, doc_lengths, tasks, w_out):
    heads, tok_dev, width = queries.shape
    n_tok = lax.axis_size("tok")
    n_head = lax.axis_size("head")
    me = lax.axis_index("tok")
    z = lax.axis_index("head")
    tokens = n_tok * tok_dev
    q_block = tokens * heads // tasks.shape[0]
    chips = n_tok // 2
    doc_most = tokens * 4 // doc_lengths.shape[0]
    back = min(chips - 1, -(-(doc_most - 1) // (2 * tok_dev)))
    out_cols = w_out.shape[1] // n_head
    flat_tasks = tasks.reshape(-1)

    turned = values.reshape(-1, width, width).transpose(0, 2, 1).reshape(values.shape)
    own = jnp.concatenate([keys, turned], axis=0)
    spans = []
    for reach in range(back, 0, -1):
        pairs = [(i, i + 2 * reach) for i in range(n_tok - 2 * reach)]
        spans.append(lax.ppermute(own, "tok", pairs))

    def column(block):
        return lax.dynamic_slice_in_dim(w_out, block * out_cols, out_cols, 1)

    w_send = jnp.concatenate([column((z ^ 1) ^ 2), column(z ^ 1)], axis=1)
    w_pass, w_keep = column(z ^ 2), column(z)
    base = (me // 2 - back) * 2 * tok_dev
    starts = [tok_dev // SUB * sum(PARTS[:at]) // sum(PARTS) for at in range(len(PARTS) + 1)]
    places = []
    for at in starts[:-1]:
        numbers = [me % 2, me * tok_dev + at * SUB, base, at * SUB]
        places.append(jnp.stack([jnp.asarray(n, jnp.int32) for n in numbers]))
    spans, w_send, w_pass, w_keep, flat_tasks, places = lax.optimization_barrier(
        (spans, w_send, w_pass, w_keep, flat_tasks, places)
    )
    swap = [(i, i ^ 1) for i in range(n_tok)]
    kvs = []
    for mine in [*spans, own]:
        kvs += [mine, lax.ppermute(mine, "tok", swap)]

    near = [(i, i ^ 1) for i in range(n_head)]
    far = [(i, i ^ 2) for i in range(n_head)]

    def project(attended):
        sent = jnp.dot(attended, w_send, preferred_element_type=jnp.float32)
        return sent.astype(jnp.bfloat16)

    def onward(attended, arrived):
        summed = jnp.dot(attended, w_pass, preferred_element_type=jnp.float32)
        summed = summed + arrived[:, :out_cols].astype(jnp.float32)
        return summed.astype(jnp.bfloat16)

    def finish(attended, arrived, crossed):
        summed = jnp.dot(attended, w_keep, preferred_element_type=jnp.float32)
        summed = summed + arrived[:, out_cols:].astype(jnp.float32)
        return (summed + crossed.astype(jnp.float32)).astype(jnp.bfloat16)

    attended, sent, arrived, other, crossed = {}, {}, {}, {}, {}
    count = len(PARTS)
    for chunk in range(count):
        place = places[chunk]
        if chunk >= 1:
            place, sent[chunk - 1] = lax.optimization_barrier((place, sent[chunk - 1]))
            arrived[chunk - 1] = lax.ppermute(sent[chunk - 1], "head", near)
        if chunk >= LAG + 1:
            late = chunk - LAG - 1
            place, other[late] = lax.optimization_barrier((place, other[late]))
            crossed[late] = lax.ppermute(other[late], "head", far)
        subs = starts[chunk + 1] - starts[chunk]
        attended[chunk] = attend(
            place, doc_lengths, flat_tasks, queries, kvs, subs, q_block
        )
        sent[chunk] = project(attended[chunk])
        if chunk >= LAG:
            late = chunk - LAG
            sent[chunk], arrived[late] = lax.optimization_barrier((sent[chunk], arrived[late]))
            other[late] = onward(attended[late], arrived[late])
            if late - 1 in crossed:
                sent[chunk], crossed[late - 1] = lax.optimization_barrier(
                    (sent[chunk], crossed[late - 1])
                )
    arrived[count - 1] = lax.ppermute(sent[count - 1], "head", near)
    for chunk in range(count):
        if chunk not in other:
            other[chunk] = onward(attended[chunk], arrived[chunk])
        if chunk not in crossed:
            crossed[chunk] = lax.ppermute(other[chunk], "head", far)
    outs = [finish(attended[c], arrived[c], crossed[c]) for c in range(count)]
    return jnp.concatenate(outs, axis=0)


def solution(mesh):
    placed = (
        P("head", "tok", None),
        P("head", "tok", None),
        P("head", "tok", None),
        P(),
        P(),
        P("head", None),
    )
    return jax.shard_map(
        local, mesh=mesh, in_specs=placed, out_specs=P("tok", "head"), check_vma=False
    )
```

```python
from functools import partial
import math

import jax
import jax.numpy as jnp
from jax import lax
from jax.experimental import pallas as pl
from jax.experimental.pallas import tpu as pltpu
from jax.sharding import PartitionSpec as P

FLOOR_SCORE = -1e30
SAFE_TOTAL = 2.0**100
KEY_TILE = 512
EDGE_TILE = 256
VMEM_BYTES = 40 * 2**20
SUB = 128
LAG = 1
PAIR = 4
PARTS = (1, 3, 3, 1)


def attend_kernel(place, lengths, tasks, q_ref, *refs, slots, subs, q_block, key_tile, edge_tile):
    kv_refs, refs = refs[:slots], refs[slots:]
    out_ref, q_buf, kv_all, acc, peak, total, s_buf, p_buf, rescale_buf, sems = refs
    heads, _, width = q_ref.shape
    shard_rows = kv_refs[0].shape[1]
    groups = heads // PAIR
    units = subs * groups
    cols = PAIR * SUB
    rows = subs * SUB
    parity = place[0]
    first_row = place[1]
    base = place[2]
    q_copy = pltpu.make_async_copy(
        q_ref.at[:, pl.ds(pl.multiple_of(place[3], SUB), rows), :], q_buf, sems.at[slots]
    )
    q_copy.start()

    last_row = first_row + rows - 1
    one_head = [
        first_row + sub * SUB + lax.broadcasted_iota(jnp.int32, (1, SUB), 1) for sub in range(subs)
    ]
    begin = [jnp.zeros((1, SUB), jnp.int32)] * subs
    begin_first = jnp.int32(0)
    begin_last = jnp.int32(0)
    start = jnp.int32(0)
    for doc in range(lengths.shape[0]):
        begin = [
            jnp.where(one >= start, jnp.maximum(old, start), old)
            for one, old in zip(one_head, begin)
        ]
        begin_first = jnp.where(first_row >= start, jnp.maximum(begin_first, start), begin_first)
        begin_last = jnp.where(last_row >= start, jnp.maximum(begin_last, start), begin_last)
        start = start + lengths[doc]

    begins, ends, lows, highs = [], [], [], []
    for sub in range(subs):
        task = ((first_row + sub * SUB) // q_block) * heads
        low = [tasks[(task + head) * 5 + 2] * q_block for head in range(heads)]
        high = [tasks[(task + head) * 5 + 3] * q_block for head in range(heads)]
        for group in range(groups):
            members = range(group * PAIR, (group + 1) * PAIR)
            begins.append(
                jnp.concatenate([jnp.maximum(begin[sub], low[m]) for m in members], axis=1)
            )
            ends.append(
                jnp.concatenate([jnp.minimum(one_head[sub], high[m] - 1) for m in members], axis=1)
            )
        lows += low
        highs += high
    low_least, low_most, high_least, high_most = lows[0], lows[0], highs[0], highs[0]
    for low, high in zip(lows[1:], highs[1:]):
        low_least, low_most = jnp.minimum(low_least, low), jnp.maximum(low_most, low)
        high_least, high_most = jnp.minimum(high_least, high), jnp.maximum(high_most, high)

    ratio = key_tile // edge_tile
    tiles = slots * shard_rows // edge_tile
    lo = jnp.clip((jnp.maximum(low_least, begin_first) - base) // edge_tile, 0, tiles)
    hi = jnp.clip(
        (jnp.minimum(high_most, last_row + 1) - base + edge_tile - 1) // edge_tile, lo, tiles
    )
    far_lo = lo // ratio
    far_hi = jnp.maximum((jnp.minimum(high_least, first_row) - base) // key_tile, far_lo)
    clear_lo = (jnp.maximum(low_most, begin_last) - base + key_tile - 1) // key_tile
    clear_lo = jnp.clip(clear_lo, far_lo, far_hi)
    near_lo = jnp.maximum(lo, far_hi * ratio)
    factor = math.log2(math.e) / math.sqrt(width)

    def reset():
        acc[...] = jnp.zeros_like(acc)
        peak[...] = jnp.full_like(peak, FLOOR_SCORE)
        total[...] = jnp.zeros_like(total)

    per_slot = shard_rows // edge_tile
    early, late = [], []
    for at in range(slots):
        slot = at // 2 * 2 + (parity if at % 2 == 0 else 1 - parity)
        copy = pltpu.make_async_copy(kv_refs[at], kv_all.at[slot], sems.at[at])
        first, last = slot * per_slot, (slot + 1) * per_slot
        soon = (near_lo < last) & (hi > first)
        used = (far_lo * ratio < last) & (hi > first)
        early.append((soon, copy))
        late.append((used & jnp.logical_not(soon), copy))
    for needed, copy in early + late:
        pl.when(needed)(copy.start)

    def wait(copies):
        for needed, copy in copies:
            pl.when(needed)(copy.wait)

    reset()
    q_copy.wait()
    wait(early)

    def sweep(count, tile_of, size, masked, fixed):
        per_shard = shard_rows // size

        def keys_of(tile):
            offset = pl.multiple_of((tile % per_shard) * size, size)
            return kv_all[tile // per_shard, 0, pl.ds(offset, size), :]

        def values_of(tile):
            offset = pl.multiple_of((tile % per_shard) * size, size)
            values = kv_all[tile // per_shard, 1, pl.ds(offset, size), :]
            values = [values[at : at + width] for at in range(0, size, width)]
            values = jnp.concatenate(values, axis=1)
            return jnp.concatenate([values, jnp.ones((16, size), jnp.bfloat16)], axis=0)

        def scores_of(keys, unit):
            sub, group = divmod(unit, groups)
            asked = q_buf[group * PAIR : (group + 1) * PAIR, sub * SUB : (sub + 1) * SUB, :]
            return lax.dot_general(
                keys,
                asked.reshape(cols, width),
                (((1,), (1,)), ((), ())),
                preferred_element_type=jnp.float32,
            )

        def gather(values, unit, weights, rescale):
            at = divmod(unit, groups)
            product = lax.dot_general(
                values, weights, (((1,), (0,)), ((), ())), preferred_element_type=jnp.float32
            )
            if fixed:
                total[at] += product[width : width + 1]
                acc[at] += product[:width]
            else:
                total[at] = total[at] * rescale + product[width : width + 1]
                acc[at] = acc[at] * rescale + product[:width]

        def step(turn, carried):
            tile = tile_of(turn)
            keys, values = keys_of(tile), values_of(tile)
            key_pos = (
                base + tile * size + lax.broadcasted_iota(jnp.int32, (size, 1), 0)
                if masked
                else None
            )
            scores = s_buf[:size]
            waiting = None
            for unit in range(units):
                at = divmod(unit, groups)
                if unit + 1 < units:
                    ahead = scores_of(keys, unit + 1)
                else:
                    ahead = scores_of(keys_of(tile_of(jnp.minimum(turn + 1, count - 1))), 0)
                if masked:
                    visible = (key_pos >= begins[unit]) & (key_pos <= ends[unit])
                    scores = jnp.where(visible, scores, FLOOR_SCORE)
                before = peak[at]
                if fixed:
                    now, rescale = before, None
                else:
                    now = jnp.maximum(before, jnp.max(scores, axis=0, keepdims=True) * factor)
                    peak[at] = now
                    rescale = jnp.exp2(before - now)
                weights = jnp.exp2(scores * factor - now).astype(jnp.bfloat16)
                if waiting is not None:
                    gather(values, unit - 1, *waiting)
                else:
                    earlier = values_of(tile_of(jnp.maximum(turn - 1, 0)))
                    gather(earlier, units - 1, p_buf[:size], rescale_buf[...])
                waiting = weights, rescale
                scores = ahead
            s_buf[:size] = scores
            p_buf[:size] = waiting[0]
            if not fixed:
                rescale_buf[...] = waiting[1]
            return carried

        def whole():
            p_buf[:size] = jnp.zeros((size, cols), jnp.bfloat16)
            rescale_buf[...] = jnp.ones_like(rescale_buf)
            s_buf[:size] = scores_of(keys_of(tile_of(0)), 0)
            lax.fori_loop(0, count, step, 0)
            gather(values_of(tile_of(count - 1)), units - 1, p_buf[:size], rescale_buf[...])

        pl.when(count > 0)(whole)

    sweep(hi - near_lo, lambda turn: near_lo + turn, edge_tile, True, False)
    wait(late)
    sweep(far_hi - clear_lo, lambda turn: clear_lo + turn, key_tile, False, True)
    sweep(clear_lo - far_lo, lambda turn: far_lo + turn, key_tile, True, True)
    in_range = jnp.min(jnp.where(total[...] < SAFE_TOTAL, 1.0, 0.0))

    @pl.when(in_range < 0.5)
    def again():
        reset()
        sweep(hi - lo, lambda turn: lo + turn, edge_tile, True, False)

    for sub in range(subs):
        for group in range(groups):
            done = (acc[sub, group] * (1.0 / total[sub, group])).astype(jnp.bfloat16).T
            for member in range(PAIR):
                head = group * PAIR + member
                out_ref[sub * SUB : (sub + 1) * SUB, head * width : (head + 1) * width] = done[
                    member * SUB : (member + 1) * SUB
                ]


def attend(place, lengths, tasks, queries, kvs, subs, q_block):
    heads, _, width = queries.shape
    shard_rows = kvs[0].shape[1]
    slots = len(kvs)
    key_tile = min(KEY_TILE, shard_rows)
    edge_tile = min(EDGE_TILE, key_tile)
    groups, cols, rows = heads // PAIR, PAIR * SUB, subs * SUB
    return pl.pallas_call(
        partial(
            attend_kernel,
            slots=slots,
            subs=subs,
            q_block=q_block,
            key_tile=key_tile,
            edge_tile=edge_tile,
        ),
        grid_spec=pltpu.PrefetchScalarGridSpec(
            num_scalar_prefetch=3,
            grid=(1,),
            in_specs=[pl.BlockSpec(memory_space=pl.ANY)] * (1 + slots),
            out_specs=pl.BlockSpec((rows, heads * width), lambda i, *_: (0, 0)),
            scratch_shapes=[
                pltpu.VMEM((heads, rows, width), jnp.bfloat16),
                pltpu.VMEM((slots, 2, shard_rows, width), jnp.bfloat16),
                pltpu.VMEM((subs, groups, width, cols), jnp.float32),
                pltpu.VMEM((subs, groups, 1, cols), jnp.float32),
                pltpu.VMEM((subs, groups, 1, cols), jnp.float32),
                pltpu.VMEM((key_tile, cols), jnp.float32),
                pltpu.VMEM((key_tile, cols), jnp.bfloat16),
                pltpu.VMEM((1, cols), jnp.float32),
                pltpu.SemaphoreType.DMA((slots + 1,)),
            ],
        ),
        out_shape=jax.ShapeDtypeStruct((rows, heads * width), jnp.bfloat16),
        compiler_params=pltpu.CompilerParams(vmem_limit_bytes=VMEM_BYTES),
        cost_estimate=pl.CostEstimate(flops=rows, bytes_accessed=rows, transcendentals=0),
    )(place, lengths, tasks, queries, *kvs)


def local(queries, keys, values, doc_lengths, tasks, w_out):
    heads, tok_dev, width = queries.shape
    n_tok = lax.axis_size("tok")
    n_head = lax.axis_size("head")
    me = lax.axis_index("tok")
    z = lax.axis_index("head")
    tokens = n_tok * tok_dev
    q_block = tokens * heads // tasks.shape[0]
    chips = n_tok // 2
    doc_most = tokens * 4 // doc_lengths.shape[0]
    back = min(chips - 1, -(-(doc_most - 1) // (2 * tok_dev)))
    out_cols = w_out.shape[1] // n_head
    flat_tasks = tasks.reshape(-1)

    turned = values.reshape(-1, width, width).transpose(0, 2, 1).reshape(values.shape)
    own = jnp.concatenate([keys, turned], axis=0)
    spans = []
    for reach in range(back, 0, -1):
        pairs = [(i, i + 2 * reach) for i in range(n_tok - 2 * reach)]
        spans.append(lax.ppermute(own, "tok", pairs))

    def column(block):
        return lax.dynamic_slice_in_dim(w_out, block * out_cols, out_cols, 1)

    w_send = jnp.concatenate([column((z ^ 1) ^ 2), column(z ^ 1)], axis=1)
    w_pass, w_keep = column(z ^ 2), column(z)
    base = (me // 2 - back) * 2 * tok_dev
    starts = [tok_dev // SUB * sum(PARTS[:at]) // sum(PARTS) for at in range(len(PARTS) + 1)]
    places = []
    for at in starts[:-1]:
        numbers = [me % 2, me * tok_dev + at * SUB, base, at * SUB]
        places.append(jnp.stack([jnp.asarray(n, jnp.int32) for n in numbers]))
    spans, w_send, w_pass, w_keep, flat_tasks, places = lax.optimization_barrier(
        (spans, w_send, w_pass, w_keep, flat_tasks, places)
    )
    swap = [(i, i ^ 1) for i in range(n_tok)]
    kvs = []
    for mine in [*spans, own]:
        kvs += [mine, lax.ppermute(mine, "tok", swap)]

    near = [(i, i ^ 1) for i in range(n_head)]
    far = [(i, i ^ 2) for i in range(n_head)]

    def project(attended):
        sent = jnp.dot(attended, w_send, preferred_element_type=jnp.float32)
        return sent.astype(jnp.bfloat16)

    def onward(attended, arrived):
        summed = jnp.dot(attended, w_pass, preferred_element_type=jnp.float32)
        summed = summed + arrived[:, :out_cols].astype(jnp.float32)
        return summed.astype(jnp.bfloat16)

    def finish(attended, arrived, crossed):
        summed = jnp.dot(attended, w_keep, preferred_element_type=jnp.float32)
        summed = summed + arrived[:, out_cols:].astype(jnp.float32)
        return (summed + crossed.astype(jnp.float32)).astype(jnp.bfloat16)

    attended, sent, arrived, other, crossed = {}, {}, {}, {}, {}
    count = len(PARTS)
    for chunk in range(count):
        place = places[chunk]
        if chunk >= 1:
            place, sent[chunk - 1] = lax.optimization_barrier((place, sent[chunk - 1]))
            arrived[chunk - 1] = lax.ppermute(sent[chunk - 1], "head", near)
        if chunk >= LAG + 1:
            late = chunk - LAG - 1
            place, other[late] = lax.optimization_barrier((place, other[late]))
            crossed[late] = lax.ppermute(other[late], "head", far)
        subs = starts[chunk + 1] - starts[chunk]
        attended[chunk] = attend(
            place, doc_lengths, flat_tasks, queries, kvs, subs, q_block
        )
        sent[chunk] = project(attended[chunk])
        if chunk >= LAG:
            late = chunk - LAG
            sent[chunk], arrived[late] = lax.optimization_barrier((sent[chunk], arrived[late]))
            other[late] = onward(attended[late], arrived[late])
            if late - 1 in crossed:
                sent[chunk], crossed[late - 1] = lax.optimization_barrier(
                    (sent[chunk], crossed[late - 1])
                )
    arrived[count - 1] = lax.ppermute(sent[count - 1], "head", near)
    for chunk in range(count):
        if chunk not in other:
            other[chunk] = onward(attended[chunk], arrived[chunk])
        if chunk not in crossed:
            crossed[chunk] = lax.ppermute(other[chunk], "head", far)
    outs = [finish(attended[c], arrived[c], crossed[c]) for c in range(count)]
    return jnp.concatenate(outs, axis=0)


def solution(mesh):
    placed = (
        P("head", "tok", None),
        P("head", "tok", None),
        P("head", "tok", None),
        P(),
        P(),
        P("head", None),
    )
    return jax.shard_map(
        local, mesh=mesh, in_specs=placed, out_specs=P("tok", "head"), check_vma=False
    )
```

```python
from functools import partial
import math

import jax
import jax.numpy as jnp
from jax import lax
from jax.experimental import pallas as pl
from jax.experimental.pallas import tpu as pltpu
from jax.sharding import PartitionSpec as P

FLOOR_SCORE = -1e30
SAFE_TOTAL = 2.0**100
KEY_TILE = 512
EDGE_TILE = 256
VMEM_BYTES = 40 * 2**20
SUB = 128
LAG = 1
PAIR = 4
PARTS = (1, 2, 2, 2, 1)


def attend_kernel(place, lengths, tasks, q_ref, *refs, slots, subs, q_block, key_tile, edge_tile):
    kv_refs, refs = refs[:slots], refs[slots:]
    out_ref, q_buf, kv_all, acc, peak, total, s_buf, p_buf, rescale_buf, sems = refs
    heads, _, width = q_ref.shape
    shard_rows = kv_refs[0].shape[1]
    groups = heads // PAIR
    units = subs * groups
    cols = PAIR * SUB
    rows = subs * SUB
    parity = place[0]
    first_row = place[1]
    base = place[2]
    q_copy = pltpu.make_async_copy(
        q_ref.at[:, pl.ds(pl.multiple_of(place[3], SUB), rows), :], q_buf, sems.at[slots]
    )
    q_copy.start()

    last_row = first_row + rows - 1
    one_head = [
        first_row + sub * SUB + lax.broadcasted_iota(jnp.int32, (1, SUB), 1) for sub in range(subs)
    ]
    begin = [jnp.zeros((1, SUB), jnp.int32)] * subs
    begin_first = jnp.int32(0)
    begin_last = jnp.int32(0)
    start = jnp.int32(0)
    for doc in range(lengths.shape[0]):
        begin = [
            jnp.where(one >= start, jnp.maximum(old, start), old)
            for one, old in zip(one_head, begin)
        ]
        begin_first = jnp.where(first_row >= start, jnp.maximum(begin_first, start), begin_first)
        begin_last = jnp.where(last_row >= start, jnp.maximum(begin_last, start), begin_last)
        start = start + lengths[doc]

    begins, ends, lows, highs = [], [], [], []
    for sub in range(subs):
        task = ((first_row + sub * SUB) // q_block) * heads
        low = [tasks[(task + head) * 5 + 2] * q_block for head in range(heads)]
        high = [tasks[(task + head) * 5 + 3] * q_block for head in range(heads)]
        for group in range(groups):
            members = range(group * PAIR, (group + 1) * PAIR)
            begins.append(
                jnp.concatenate([jnp.maximum(begin[sub], low[m]) for m in members], axis=1)
            )
            ends.append(
                jnp.concatenate([jnp.minimum(one_head[sub], high[m] - 1) for m in members], axis=1)
            )
        lows += low
        highs += high
    low_least, low_most, high_least, high_most = lows[0], lows[0], highs[0], highs[0]
    for low, high in zip(lows[1:], highs[1:]):
        low_least, low_most = jnp.minimum(low_least, low), jnp.maximum(low_most, low)
        high_least, high_most = jnp.minimum(high_least, high), jnp.maximum(high_most, high)

    ratio = key_tile // edge_tile
    tiles = slots * shard_rows // edge_tile
    lo = jnp.clip((jnp.maximum(low_least, begin_first) - base) // edge_tile, 0, tiles)
    hi = jnp.clip(
        (jnp.minimum(high_most, last_row + 1) - base + edge_tile - 1) // edge_tile, lo, tiles
    )
    far_lo = lo // ratio
    far_hi = jnp.maximum((jnp.minimum(high_least, first_row) - base) // key_tile, far_lo)
    clear_lo = (jnp.maximum(low_most, begin_last) - base + key_tile - 1) // key_tile
    clear_lo = jnp.clip(clear_lo, far_lo, far_hi)
    near_lo = jnp.maximum(lo, far_hi * ratio)
    factor = math.log2(math.e) / math.sqrt(width)

    def reset():
        acc[...] = jnp.zeros_like(acc)
        peak[...] = jnp.full_like(peak, FLOOR_SCORE)
        total[...] = jnp.zeros_like(total)

    per_slot = shard_rows // edge_tile
    early, late = [], []
    for at in range(slots):
        slot = at // 2 * 2 + (parity if at % 2 == 0 else 1 - parity)
        copy = pltpu.make_async_copy(kv_refs[at], kv_all.at[slot], sems.at[at])
        first, last = slot * per_slot, (slot + 1) * per_slot
        soon = (near_lo < last) & (hi > first)
        used = (far_lo * ratio < last) & (hi > first)
        early.append((soon, copy))
        late.append((used & jnp.logical_not(soon), copy))
    for needed, copy in early + late:
        pl.when(needed)(copy.start)

    def wait(copies):
        for needed, copy in copies:
            pl.when(needed)(copy.wait)

    reset()
    q_copy.wait()
    wait(early)

    def sweep(count, tile_of, size, masked, fixed):
        per_shard = shard_rows // size

        def keys_of(tile):
            offset = pl.multiple_of((tile % per_shard) * size, size)
            return kv_all[tile // per_shard, 0, pl.ds(offset, size), :]

        def values_of(tile):
            offset = pl.multiple_of((tile % per_shard) * size, size)
            values = kv_all[tile // per_shard, 1, pl.ds(offset, size), :]
            values = [values[at : at + width] for at in range(0, size, width)]
            values = jnp.concatenate(values, axis=1)
            return jnp.concatenate([values, jnp.ones((16, size), jnp.bfloat16)], axis=0)

        def scores_of(keys, unit):
            sub, group = divmod(unit, groups)
            asked = q_buf[group * PAIR : (group + 1) * PAIR, sub * SUB : (sub + 1) * SUB, :]
            return lax.dot_general(
                keys,
                asked.reshape(cols, width),
                (((1,), (1,)), ((), ())),
                preferred_element_type=jnp.float32,
            )

        def gather(values, unit, weights, rescale):
            at = divmod(unit, groups)
            product = lax.dot_general(
                values, weights, (((1,), (0,)), ((), ())), preferred_element_type=jnp.float32
            )
            if fixed:
                total[at] += product[width : width + 1]
                acc[at] += product[:width]
            else:
                total[at] = total[at] * rescale + product[width : width + 1]
                acc[at] = acc[at] * rescale + product[:width]

        def step(turn, carried):
            tile = tile_of(turn)
            keys, values = keys_of(tile), values_of(tile)
            key_pos = (
                base + tile * size + lax.broadcasted_iota(jnp.int32, (size, 1), 0)
                if masked
                else None
            )
            scores = s_buf[:size]
            waiting = None
            for unit in range(units):
                at = divmod(unit, groups)
                if unit + 1 < units:
                    ahead = scores_of(keys, unit + 1)
                else:
                    ahead = scores_of(keys_of(tile_of(jnp.minimum(turn + 1, count - 1))), 0)
                if masked:
                    visible = (key_pos >= begins[unit]) & (key_pos <= ends[unit])
                    scores = jnp.where(visible, scores, FLOOR_SCORE)
                before = peak[at]
                if fixed:
                    now, rescale = before, None
                else:
                    now = jnp.maximum(before, jnp.max(scores, axis=0, keepdims=True) * factor)
                    peak[at] = now
                    rescale = jnp.exp2(before - now)
                weights = jnp.exp2(scores * factor - now).astype(jnp.bfloat16)
                if waiting is not None:
                    gather(values, unit - 1, *waiting)
                else:
                    earlier = values_of(tile_of(jnp.maximum(turn - 1, 0)))
                    gather(earlier, units - 1, p_buf[:size], rescale_buf[...])
                waiting = weights, rescale
                scores = ahead
            s_buf[:size] = scores
            p_buf[:size] = waiting[0]
            if not fixed:
                rescale_buf[...] = waiting[1]
            return carried

        def whole():
            p_buf[:size] = jnp.zeros((size, cols), jnp.bfloat16)
            rescale_buf[...] = jnp.ones_like(rescale_buf)
            s_buf[:size] = scores_of(keys_of(tile_of(0)), 0)
            lax.fori_loop(0, count, step, 0)
            gather(values_of(tile_of(count - 1)), units - 1, p_buf[:size], rescale_buf[...])

        pl.when(count > 0)(whole)

    sweep(hi - near_lo, lambda turn: near_lo + turn, edge_tile, True, False)
    wait(late)
    sweep(far_hi - clear_lo, lambda turn: clear_lo + turn, key_tile, False, True)
    sweep(clear_lo - far_lo, lambda turn: far_lo + turn, key_tile, True, True)
    in_range = jnp.min(jnp.where(total[...] < SAFE_TOTAL, 1.0, 0.0))

    @pl.when(in_range < 0.5)
    def again():
        reset()
        sweep(hi - lo, lambda turn: lo + turn, edge_tile, True, False)

    for sub in range(subs):
        for group in range(groups):
            done = (acc[sub, group] * (1.0 / total[sub, group])).astype(jnp.bfloat16).T
            for member in range(PAIR):
                head = group * PAIR + member
                out_ref[sub * SUB : (sub + 1) * SUB, head * width : (head + 1) * width] = done[
                    member * SUB : (member + 1) * SUB
                ]


def attend(place, lengths, tasks, queries, kvs, subs, q_block):
    heads, _, width = queries.shape
    shard_rows = kvs[0].shape[1]
    slots = len(kvs)
    key_tile = min(KEY_TILE, shard_rows)
    edge_tile = min(EDGE_TILE, key_tile)
    groups, cols, rows = heads // PAIR, PAIR * SUB, subs * SUB
    return pl.pallas_call(
        partial(
            attend_kernel,
            slots=slots,
            subs=subs,
            q_block=q_block,
            key_tile=key_tile,
            edge_tile=edge_tile,
        ),
        grid_spec=pltpu.PrefetchScalarGridSpec(
            num_scalar_prefetch=3,
            grid=(1,),
            in_specs=[pl.BlockSpec(memory_space=pl.ANY)] * (1 + slots),
            out_specs=pl.BlockSpec((rows, heads * width), lambda i, *_: (0, 0)),
            scratch_shapes=[
                pltpu.VMEM((heads, rows, width), jnp.bfloat16),
                pltpu.VMEM((slots, 2, shard_rows, width), jnp.bfloat16),
                pltpu.VMEM((subs, groups, width, cols), jnp.float32),
                pltpu.VMEM((subs, groups, 1, cols), jnp.float32),
                pltpu.VMEM((subs, groups, 1, cols), jnp.float32),
                pltpu.VMEM((key_tile, cols), jnp.float32),
                pltpu.VMEM((key_tile, cols), jnp.bfloat16),
                pltpu.VMEM((1, cols), jnp.float32),
                pltpu.SemaphoreType.DMA((slots + 1,)),
            ],
        ),
        out_shape=jax.ShapeDtypeStruct((rows, heads * width), jnp.bfloat16),
        compiler_params=pltpu.CompilerParams(vmem_limit_bytes=VMEM_BYTES),
        cost_estimate=pl.CostEstimate(flops=rows, bytes_accessed=rows, transcendentals=0),
    )(place, lengths, tasks, queries, *kvs)


def local(queries, keys, values, doc_lengths, tasks, w_out):
    heads, tok_dev, width = queries.shape
    n_tok = lax.axis_size("tok")
    n_head = lax.axis_size("head")
    me = lax.axis_index("tok")
    z = lax.axis_index("head")
    tokens = n_tok * tok_dev
    q_block = tokens * heads // tasks.shape[0]
    chips = n_tok // 2
    doc_most = tokens * 4 // doc_lengths.shape[0]
    back = min(chips - 1, -(-(doc_most - 1) // (2 * tok_dev)))
    out_cols = w_out.shape[1] // n_head
    flat_tasks = tasks.reshape(-1)

    turned = values.reshape(-1, width, width).transpose(0, 2, 1).reshape(values.shape)
    own = jnp.concatenate([keys, turned], axis=0)
    spans = []
    for reach in range(back, 0, -1):
        pairs = [(i, i + 2 * reach) for i in range(n_tok - 2 * reach)]
        spans.append(lax.ppermute(own, "tok", pairs))

    def column(block):
        return lax.dynamic_slice_in_dim(w_out, block * out_cols, out_cols, 1)

    w_send = jnp.concatenate([column((z ^ 1) ^ 2), column(z ^ 1)], axis=1)
    w_pass, w_keep = column(z ^ 2), column(z)
    base = (me // 2 - back) * 2 * tok_dev
    starts = [tok_dev // SUB * sum(PARTS[:at]) // sum(PARTS) for at in range(len(PARTS) + 1)]
    places = []
    for at in starts[:-1]:
        numbers = [me % 2, me * tok_dev + at * SUB, base, at * SUB]
        places.append(jnp.stack([jnp.asarray(n, jnp.int32) for n in numbers]))
    spans, w_send, w_pass, w_keep, flat_tasks, places = lax.optimization_barrier(
        (spans, w_send, w_pass, w_keep, flat_tasks, places)
    )
    swap = [(i, i ^ 1) for i in range(n_tok)]
    kvs = []
    for mine in [*spans, own]:
        kvs += [mine, lax.ppermute(mine, "tok", swap)]

    near = [(i, i ^ 1) for i in range(n_head)]
    far = [(i, i ^ 2) for i in range(n_head)]

    def project(attended):
        sent = jnp.dot(attended, w_send, preferred_element_type=jnp.float32)
        return sent.astype(jnp.bfloat16)

    def onward(attended, arrived):
        summed = jnp.dot(attended, w_pass, preferred_element_type=jnp.float32)
        summed = summed + arrived[:, :out_cols].astype(jnp.float32)
        return summed.astype(jnp.bfloat16)

    def finish(attended, arrived, crossed):
        summed = jnp.dot(attended, w_keep, preferred_element_type=jnp.float32)
        summed = summed + arrived[:, out_cols:].astype(jnp.float32)
        return (summed + crossed.astype(jnp.float32)).astype(jnp.bfloat16)

    attended, sent, arrived, other, crossed = {}, {}, {}, {}, {}
    count = len(PARTS)
    for chunk in range(count):
        place = places[chunk]
        if chunk >= 1:
            place, sent[chunk - 1] = lax.optimization_barrier((place, sent[chunk - 1]))
            arrived[chunk - 1] = lax.ppermute(sent[chunk - 1], "head", near)
        if chunk >= LAG + 1:
            late = chunk - LAG - 1
            place, other[late] = lax.optimization_barrier((place, other[late]))
            crossed[late] = lax.ppermute(other[late], "head", far)
        subs = starts[chunk + 1] - starts[chunk]
        attended[chunk] = attend(
            place, doc_lengths, flat_tasks, queries, kvs, subs, q_block
        )
        sent[chunk] = project(attended[chunk])
        if chunk >= LAG:
            late = chunk - LAG
            sent[chunk], arrived[late] = lax.optimization_barrier((sent[chunk], arrived[late]))
            other[late] = onward(attended[late], arrived[late])
            if late - 1 in crossed and chunk < count - 1:
                sent[chunk], crossed[late - 1] = lax.optimization_barrier(
                    (sent[chunk], crossed[late - 1])
                )
    arrived[count - 1] = lax.ppermute(sent[count - 1], "head", near)
    for chunk in range(count):
        if chunk not in other:
            other[chunk] = onward(attended[chunk], arrived[chunk])
        if chunk not in crossed:
            crossed[chunk] = lax.ppermute(other[chunk], "head", far)
    outs = [finish(attended[c], arrived[c], crossed[c]) for c in range(count)]
    return jnp.concatenate(outs, axis=0)


def solution(mesh):
    placed = (
        P("head", "tok", None),
        P("head", "tok", None),
        P("head", "tok", None),
        P(),
        P(),
        P("head", None),
    )
    return jax.shard_map(
        local, mesh=mesh, in_specs=placed, out_specs=P("tok", "head"), check_vma=False
    )
```
